32 devices in a mesh: dp: 8 (over z, x), tensor: 4 (over y, core).
Axes of the slice: x: 2, y: 2, z: 4, core: 2. Of those that a mesh axis runs over, the one named last changes fastest.
Arguments:
- latents: bfloat16 [16, 1024, 1408], P('dp', 'tensor'), may hold values from -6 to 6
- skip_input: bfloat16 [16, 1024, 1408], P('dp', 'tensor'), may hold values from -6 to 6
- text_states: bfloat16 [16, 333, 1024], P('dp'), may hold values from -6 to 6
- timesteps: int32 [16], P('dp'), may hold values from 0 to 999
- patch_order: int32 [1024], replicated, may hold values from 0 to 1023, each once
- out_grad: float32 [16, 1024, 1408], P('dp', 'tensor'), may hold values from -6 to 6
- head_inputs: float32 [1408, 4, 1408], P('dp', None, 'tensor'), may hold values from -0.15625 to 0.15625
- first_head_inputs: float32 [1408, 4, 1408], P('dp', None, 'tensor'), may hold values from -24 to 24
- second_head_inputs: float32 [1408, 4, 1408], P('dp', None, 'tensor'), may hold values from 163.84 to 655.36
- text_inputs: float32 [1024, 2, 1408], P('dp', None, 'tensor'), may hold values from -0.1875 to 0.1875
- first_text_inputs: float32 [1024, 2, 1408], P('dp', None, 'tensor'), may hold values from -24 to 24
- second_text_inputs: float32 [1024, 2, 1408], P('dp', None, 'tensor'), may hold values from 163.84 to 655.36
- head_outputs: float32 [2, 1408, 1408], P(None, 'tensor', 'dp'), may hold values from -1.25 to 1.25
- first_head_outputs: float32 [2, 1408, 1408], P(None, 'tensor', 'dp'), may hold values from -24 to 24
- second_head_outputs: float32 [2, 1408, 1408], P(None, 'tensor', 'dp'), may hold values from 2.56 to 10.24
- mlp_inner: float32 [1408, 6144], P('dp', 'tensor'), may hold values from -0.15625 to 0.15625
- first_mlp_inner: float32 [1408, 6144], P('dp', 'tensor'), may hold values from -24 to 24
- second_mlp_inner: float32 [1408, 6144], P('dp', 'tensor'), may hold values from 3.2768 to 13.1072
- mlp_outer: float32 [6144, 1408], P('tensor', 'dp'), may hold values from -0.078125 to 0.078125
- first_mlp_outer: float32 [6144, 1408], P('tensor', 'dp'), may hold values from -24 to 24
- second_mlp_outer: float32 [6144, 1408], P('tensor', 'dp'), may hold values from 10.24 to 40.96
- skip_linear: float32 [2816, 1408], P('dp'), may hold values from -0.109375 to 0.109375
- first_skip_linear: float32 [2816, 1408], P('dp'), may hold values from -24 to 24
- second_skip_linear: float32 [2816, 1408], P('dp'), may hold values from 163.84 to 655.36
- shift_linear: float32 [1408, 1408], P('dp'), may hold values from -0.15625 to 0.15625
- first_shift_linear: float32 [1408, 1408], P('dp'), may hold values from -24 to 24
- second_shift_linear: float32 [1408, 1408], P('dp'), may hold values from 163.84 to 655.36
- row_gains: float32 [5, 1408], replicated, may hold values from 0.5 to 1.5
- first_row_gains: float32 [5, 1408], replicated, may hold values from -24 to 24
- second_row_gains: float32 [5, 1408], replicated, may hold values from 163.84 to 655.36
- head_gains: float32 [4, 88], replicated, may hold values from 0.25 to 1.75
- first_head_gains: float32 [4, 88], replicated, may hold values from -96 to 96
- second_head_gains: float32 [4, 88], replicated, may hold values from 2621.44 to 10485.76
Outputs:
- block_out: float32 [16, 1024, 1408], P('dp', 'tensor')
- grad_latents: float32 [16, 1024, 1408], P('dp', 'tensor')
- grad_skip_input: float32 [16, 1024, 1408], P('dp', 'tensor')
- grad_head_inputs: float32 [1408, 4, 1408], P('dp', None, 'tensor')
- next_first_head_inputs: float32 [1408, 4, 1408], P('dp', None, 'tensor')
- next_second_head_inputs: float32 [1408, 4, 1408], P('dp', None, 'tensor')
- new_head_inputs: float32 [1408, 4, 1408], P('dp', None, 'tensor')
- grad_text_inputs: float32 [1024, 2, 1408], P('dp', None, 'tensor')
- next_first_text_inputs: float32 [1024, 2, 1408], P('dp', None, 'tensor')
- next_second_text_inputs: float32 [1024, 2, 1408], P('dp', None, 'tensor')
- new_text_inputs: float32 [1024, 2, 1408], P('dp', None, 'tensor')
- grad_head_outputs: float32 [2, 1408, 1408], P(None, 'tensor', 'dp')
- next_first_head_outputs: float32 [2, 1408, 1408], P(None, 'tensor', 'dp')
- next_second_head_outputs: float32 [2, 1408, 1408], P(None, 'tensor', 'dp')
- new_head_outputs: float32 [2, 1408, 1408], P(None, 'tensor', 'dp')
- grad_mlp_inner: float32 [1408, 6144], P('dp', 'tensor')
- next_first_mlp_inner: float32 [1408, 6144], P('dp', 'tensor')
- next_second_mlp_inner: float32 [1408, 6144], P('dp', 'tensor')
- new_mlp_inner: float32 [1408, 6144], P('dp', 'tensor')
- grad_mlp_outer: float32 [6144, 1408], P('tensor', 'dp')
- next_first_mlp_outer: float32 [6144, 1408], P('tensor', 'dp')
- next_second_mlp_outer: float32 [6144, 1408], P('tensor', 'dp')
- new_mlp_outer: float32 [6144, 1408], P('tensor', 'dp')
- grad_skip_linear: float32 [2816, 1408], P('dp')
- next_first_skip_linear: float32 [2816, 1408], P('dp')
- next_second_skip_linear: float32 [2816, 1408], P('dp')
- new_skip_linear: float32 [2816, 1408], P('dp')
- grad_shift_linear: float32 [1408, 1408], P('dp')
- next_first_shift_linear: float32 [1408, 1408], P('dp')
- next_second_shift_linear: float32 [1408, 1408], P('dp')
- new_shift_linear: float32 [1408, 1408], P('dp')
- grad_row_gains: float32 [5, 1408], replicated
- next_first_row_gains: float32 [5, 1408], replicated
- next_second_row_gains: float32 [5, 1408], replicated
- new_row_gains: float32 [5, 1408], replicated
- grad_head_gains: float32 [4, 88], replicated
- next_first_head_gains: float32 [4, 88], replicated
- next_second_head_gains: float32 [4, 88], replicated
- new_head_gains: float32 [4, 88], replicated
- weight_norms: float32 [12], replicated
- ratio_norms: float32 [12], replicated
The draws below stay inside these ranges and needn't reach their ends.
Inputs may be any that keep to these rules, and one draw needn't show every extreme that they name: `patch_order`: each of the 1024 grid cells once; cell c lies at row c // 32, column c % 32.
All inputs are finite; a program needn't handle non-finite values.
Results may differ from the reference program's by a relative error of at most 0.018.
Values may be sent and summed in bfloat16 or wider, within the bound.
No kernel may reach another device: no remote copies, remote signals or barrier semaphores. Data moves between devices by JAX's collectives and lax.ppermute only.
A program may use at most 320 MiB of HBM per device.

```python
import math
import jax
import jax.numpy as jnp
from jax import lax

D = 1408
H = 16
HD = 88
FF = 6144
TD = 1024
TXT = 333
GRID = 32
L = 1024
B = 16


def with_ends(entries, own_key, low, largest):
    longest = entries.shape.index(max(entries.shape))
    spots = []
    for shift in (0, 1):
        where = [jax.random.randint(jax.random.fold_in(own_key, axis), (), 0, length) for axis, length in enumerate(entries.shape)]
        where[longest] = (where[longest] + shift) % entries.shape[longest]
        spots.append(tuple(where))
    return entries.at[spots[0]].set(low).at[spots[1]].set(largest)


def level_of(stream_key, extent, split, smallest, top_value):
    gain, own = 1.0, jax.random.fold_in(stream_key, 6)
    for axis_at, parts in split:
        heights = jnp.exp(jax.random.uniform(jax.random.fold_in(own, axis_at), (parts,), jnp.float32, smallest / len(split), top_value / len(split)))
        gain = gain * jnp.repeat(heights, extent[axis_at] // parts).reshape([-1 if axis == axis_at else 1 for axis in range(len(extent))])
    return gain


def noise(stream_key, extent, width, most, pieces=(), dtype=jnp.bfloat16):
    values = jax.random.normal(stream_key, extent, jnp.float32) * width
    if len(pieces) > 0:
        values = level_of(stream_key, extent, pieces, -0.22, 0.18) * values
    return jnp.clip(values, min=-most, max=most).astype(dtype)


def setup_inputs(seed: int = 0) -> dict:
    seeds = jax.random.split(jax.random.key(seed), 34)
    latents = noise(seeds[0], (B, L, D), 1.0, 6.0, ((0, 8), (1, 4)))
    skip_input = noise(seeds[1], (B, L, D), 1.0, 6.0, ((0, 8), (1, 4)))
    text_states = noise(seeds[2], (B, TXT, TD), 1.0, 6.0, ((0, 8),))
    timesteps = with_ends(jax.random.randint(seeds[3], (B,), 0, 1000), jax.random.fold_in(seeds[3], 1), 0, 999).astype(jnp.int32)
    patch_order = jax.random.permutation(seeds[4], L).astype(jnp.int32)
    out_grad = noise(seeds[5], (B, L, D), 1.0, 6.0, ((0, 8), (1, 4)), jnp.float32)
    head_inputs = noise(seeds[6], (D, 4, D), D ** -0.5, 0.15625, ((0, 8), (2, 4)), jnp.float32)
    first_head_inputs = noise(seeds[7], (D, 4, D), (0.03 * (B * L) ** 0.5), 24.0, ((0, 8), (2, 4)), jnp.float32)
    second_head_inputs = jnp.clip(jnp.exp(math.log(655.36) - 1.3862944 * jax.random.uniform(seeds[8], (D, 4, D), jnp.float32) ** level_of(seeds[8], (D, 4, D), ((0, 8), (2, 4)), -0.2, 0.2)), 163.84, 655.36)
    text_inputs = noise(seeds[9], (TD, 2, D), TD ** -0.5, 0.1875, ((0, 8), (2, 4)), jnp.float32)
    first_text_inputs = noise(seeds[10], (TD, 2, D), (0.03 * (B * L) ** 0.5), 24.0, ((0, 8), (2, 4)), jnp.float32)
    second_text_inputs = jnp.clip(jnp.exp(math.log(655.36) - 1.3862944 * jax.random.uniform(seeds[11], (TD, 2, D), jnp.float32) ** level_of(seeds[11], (TD, 2, D), ((0, 8), (2, 4)), -0.2, 0.2)), 163.84, 655.36)
    head_outputs = noise(seeds[12], (2, D, D), (max(D * 16 // L, 1)) ** -0.5, 1.25, ((1, 4), (2, 8)), jnp.float32)
    first_head_outputs = noise(seeds[13], (2, D, D), (0.03 * (B * L) ** 0.5), 24.0, ((1, 4), (2, 8)), jnp.float32)
    second_head_outputs = jnp.clip(jnp.exp(math.log(10.24) - 1.3862944 * jax.random.uniform(seeds[14], (2, D, D), jnp.float32) ** level_of(seeds[14], (2, D, D), ((1, 4), (2, 8)), -0.2, 0.2)), 2.56, 10.24)
    mlp_inner = noise(seeds[15], (D, FF), D ** -0.5, 0.15625, ((0, 8), (1, 4)), jnp.float32)
    first_mlp_inner = noise(seeds[16], (D, FF), (0.03 * (B * L) ** 0.5), 24.0, ((0, 8), (1, 4)), jnp.float32)
    second_mlp_inner = jnp.clip(jnp.exp(math.log(13.1072) - 1.3862944 * jax.random.uniform(seeds[17], (D, FF), jnp.float32) ** level_of(seeds[17], (D, FF), ((0, 8), (1, 4)), -0.2, 0.2)), 3.2768, 13.1072)
    mlp_outer = noise(seeds[18], (FF, D), FF ** -0.5, 0.078125, ((0, 4), (1, 8)), jnp.float32)
    first_mlp_outer = noise(seeds[19], (FF, D), (0.03 * (B * L) ** 0.5), 24.0, ((0, 4), (1, 8)), jnp.float32)
    second_mlp_outer = jnp.clip(jnp.exp(math.log(40.96) - 1.3862944 * jax.random.uniform(seeds[20], (FF, D), jnp.float32) ** level_of(seeds[20], (FF, D), ((0, 4), (1, 8)), -0.2, 0.2)), 10.24, 40.96)
    skip_linear = noise(seeds[21], (2 * D, D), (2 * D) ** -0.5, 0.109375, ((0, 8),), jnp.float32)
    first_skip_linear = noise(seeds[22], (2 * D, D), (0.03 * (B * L) ** 0.5), 24.0, ((0, 8),), jnp.float32)
    second_skip_linear = jnp.clip(jnp.exp(math.log(655.36) - 1.3862944 * jax.random.uniform(seeds[23], (2 * D, D), jnp.float32) ** level_of(seeds[23], (2 * D, D), ((0, 8),), -0.2, 0.2)), 163.84, 655.36)
    shift_linear = noise(seeds[24], (D, D), D ** -0.5, 0.15625, ((0, 8),), jnp.float32)
    first_shift_linear = noise(seeds[25], (D, D), (0.03 * (B * L) ** 0.5), 24.0, ((0, 8),), jnp.float32)
    second_shift_linear = jnp.clip(jnp.exp(math.log(655.36) - 1.3862944 * jax.random.uniform(seeds[26], (D, D), jnp.float32) ** level_of(seeds[26], (D, D), ((0, 8),), -0.2, 0.2)), 163.84, 655.36)
    row_gains = jnp.clip(1.0 + 0.1 * jax.random.normal(seeds[27], (5, D), jnp.float32), 0.5, 1.5)
    first_row_gains = noise(seeds[28], (5, D), (0.03 * (B * L) ** 0.5), 24.0, (), jnp.float32)
    second_row_gains = jnp.clip(jnp.exp(jax.random.uniform(seeds[29], (5, D), jnp.float32, math.log(163.84), math.log(655.36))), 163.84, 655.36)
    head_gains = jnp.clip(1.0 + 0.15 * jax.random.normal(seeds[30], (4, HD), jnp.float32), 0.25, 1.75)
    first_head_gains = noise(seeds[31], (4, HD), (0.03 * (B * L * H) ** 0.5), 96.0, (), jnp.float32)
    second_head_gains = jnp.clip(jnp.exp(jax.random.uniform(seeds[32], (4, HD), jnp.float32, math.log(2621.44), math.log(10485.76))), 2621.44, 10485.76)
    return {"latents": latents, "skip_input": skip_input, "text_states": text_states, "timesteps": timesteps, "patch_order": patch_order, "out_grad": out_grad, "head_inputs": head_inputs, "first_head_inputs": first_head_inputs, "second_head_inputs": second_head_inputs, "text_inputs": text_inputs, "first_text_inputs": first_text_inputs, "second_text_inputs": second_text_inputs, "head_outputs": head_outputs, "first_head_outputs": first_head_outputs, "second_head_outputs": second_head_outputs, "mlp_inner": mlp_inner, "first_mlp_inner": first_mlp_inner, "second_mlp_inner": second_mlp_inner, "mlp_outer": mlp_outer, "first_mlp_outer": first_mlp_outer, "second_mlp_outer": second_mlp_outer, "skip_linear": skip_linear, "first_skip_linear": first_skip_linear, "second_skip_linear": second_skip_linear, "shift_linear": shift_linear, "first_shift_linear": first_shift_linear, "second_shift_linear": second_shift_linear, "row_gains": row_gains, "first_row_gains": first_row_gains, "second_row_gains": second_row_gains, "head_gains": head_gains, "first_head_gains": first_head_gains, "second_head_gains": second_head_gains}


@jax.custom_vjp
def low(v):
    return lax.optimization_barrier(v.astype(jnp.bfloat16)).astype(jnp.float32)

@jax.custom_vjp
def low_back(v):
    return v

def low_keep(v):
    return (low(v), None)

def low_pass(kept, grad):
    return (grad,)

def back_keep(v):
    return (v, None)

def back_low(kept, grad):
    return (low(grad),)
low.defvjp(low_keep, low_pass)
low_back.defvjp(back_keep, back_low)
norm_eps = 1e-06
beta_one = 0.9
beta_two = 0.999
adam_eps = 1e-06
decay_rate = 0.01
learn_rate = 0.3
step_count = 10.0
highest = lax.Precision.HIGHEST

def matmul(left, right):
    return jnp.dot(left, right, precision=highest, preferred_element_type=jnp.float32)

def norm_rows(values, factor):
    center = values - lax.optimization_barrier(jnp.mean(values, axis=-1, keepdims=True))
    spread = lax.optimization_barrier(jnp.mean(center * center, axis=-1, keepdims=True))
    return center * lax.rsqrt(spread + norm_eps) * factor

def rotate_pairs(values, cosines, sines):
    layout = values.shape
    paired = values.reshape(layout[:-1] + (layout[-1] // 2, 2))
    turned = jnp.stack([-paired[..., 1], paired[..., 0]], -1).reshape(layout)
    return values * cosines + turned * sines

def rotary_tables(patch_order):
    places = patch_order.astype(jnp.int32)
    grid_row = (places // GRID).astype(jnp.float32)
    grid_col = (places % GRID).astype(jnp.float32)
    quarter = HD // 4
    spacing = 10000.0 ** (-jnp.arange(quarter).astype(jnp.float32) / quarter)
    row_angle = jnp.repeat(grid_row[:, None] * spacing[None, :], 2, axis=1)
    col_angle = jnp.repeat(grid_col[:, None] * spacing[None, :], 2, axis=1)
    angles = jnp.concatenate([row_angle, col_angle], 1)
    return (jnp.cos(angles)[:, None, :], jnp.sin(angles)[:, None, :])

def time_embed(timesteps):
    half_width = D // 2
    spacing = jnp.exp(-math.log(10000.0) * jnp.arange(half_width).astype(jnp.float32) / half_width)
    angles = timesteps.astype(jnp.float32)[:, None] * spacing[None, :]
    return jnp.concatenate([jnp.cos(angles), jnp.sin(angles)], -1)

def split_heads(pre):
    return low_back(pre).reshape(pre.shape[0], -1, HD)

def attention(query, keys, values):
    scores = low_back(jnp.einsum('qhd,khd->hqk', query, keys, precision=highest) * HD ** (-0.5))
    chances = low(jax.nn.softmax(scores, axis=-1))
    mixed = jnp.einsum('hqk,khd->qhd', chances, values, precision=highest)
    mixed = low(low_back(mixed))
    return mixed.reshape(mixed.shape[0], -1)

def forward(weights, gains, latent, skip_part, text_part, cond, cosines, sines):
    head_mats, text_mats, out_mats, inner_mat, outer_mat, skip_mat, shift_mat = [low(item) for item in weights]
    row_gains, head_gains = gains
    joined = jnp.concatenate([latent, skip_part], -1)
    normed = low(norm_rows(joined, jnp.concatenate([row_gains[0], row_gains[1]])))
    hidden = low_back(matmul(normed, skip_mat))
    shift = matmul(low(jax.nn.silu(cond))[None, :], shift_mat)
    attn_input = low(norm_rows(hidden, row_gains[2]) + shift)
    query = low(rotate_pairs(norm_rows(split_heads(matmul(attn_input, head_mats[:, 0, :])), head_gains[0]), cosines, sines))
    keys = low(rotate_pairs(norm_rows(split_heads(matmul(attn_input, head_mats[:, 1, :])), head_gains[1]), cosines, sines))
    values = low(split_heads(matmul(attn_input, head_mats[:, 2, :])))
    after_self = hidden + low_back(matmul(attention(query, keys, values), out_mats[0]))
    cross_input = low(norm_rows(after_self, row_gains[3]))
    cross_query = low(rotate_pairs(norm_rows(split_heads(matmul(cross_input, head_mats[:, 3, :])), head_gains[2]), cosines, sines))
    text_keys = low(norm_rows(split_heads(matmul(text_part, text_mats[:, 0, :])), head_gains[3]))
    text_values = low(split_heads(matmul(text_part, text_mats[:, 1, :])))
    after_cross = after_self + low_back(matmul(attention(cross_query, text_keys, text_values), out_mats[1]))
    mlp_input = low(norm_rows(after_cross, row_gains[4]))
    activated = low(jax.nn.gelu(low_back(matmul(mlp_input, inner_mat)), approximate=True))
    return after_cross + low_back(matmul(activated, outer_mat))

def lamb_parts(master, first, second, grad, axes):
    next_first = beta_one * first + (1.0 - beta_one) * grad
    next_second = beta_two * second + (1.0 - beta_two) * grad * grad
    ratio = next_first / (1.0 - beta_one ** step_count) / (jnp.sqrt(next_second / (1.0 - beta_two ** step_count)) + adam_eps) + decay_rate * master
    weight_norm = jnp.sqrt(lax.optimization_barrier(jnp.sum(master * master, axis=axes, keepdims=True)))
    ratio_norm = jnp.sqrt(lax.optimization_barrier(jnp.sum(ratio * ratio, axis=axes, keepdims=True)))
    renewed = master - learn_rate * (weight_norm / ratio_norm) * ratio
    return (grad, next_first, next_second, renewed, weight_norm.reshape(-1), ratio_norm.reshape(-1))

def reference(latents, skip_input, text_states, timesteps, patch_order, out_grad, head_inputs, first_head_inputs, second_head_inputs, text_inputs, first_text_inputs, second_text_inputs, head_outputs, first_head_outputs, second_head_outputs, mlp_inner, first_mlp_inner, second_mlp_inner, mlp_outer, first_mlp_outer, second_mlp_outer, skip_linear, first_skip_linear, second_skip_linear, shift_linear, first_shift_linear, second_shift_linear, row_gains, first_row_gains, second_row_gains, head_gains, first_head_gains, second_head_gains):
    weights = (head_inputs, text_inputs, head_outputs, mlp_inner, mlp_outer, skip_linear, shift_linear)
    gains = (row_gains, head_gains)
    cosines, sines = rotary_tables(patch_order)
    conditions = time_embed(timesteps)

    def one_latent(carry, items):
        latent, skip_part, text_part, cond, cotangent = items
        text_value = text_part.astype(jnp.float32)

        def run(weights_in, gains_in, latent_in, skip_in):
            return forward(weights_in, gains_in, latent_in, skip_in, text_value, cond, cosines, sines)
        result, pull = jax.vjp(run, weights, gains, latent.astype(jnp.float32), skip_part.astype(jnp.float32))
        weight_grads, gain_grads, latent_grad, skip_grad = pull(cotangent)
        carry = jax.tree.map(lambda left, right: left + right, carry, (weight_grads, gain_grads))
        return (carry, (result, latent_grad, skip_grad))
    zeroed = jax.tree.map(jnp.zeros_like, (weights, gains))
    totals, (block_out, grad_latents, grad_skip_input) = lax.scan(one_latent, zeroed, (latents, skip_input, text_states, conditions, out_grad))
    weight_sums, gain_sums = totals
    head_in_grad, head_in_first, head_in_second, head_in_new, head_in_wn, head_in_rn = lamb_parts(head_inputs, first_head_inputs, second_head_inputs, weight_sums[0], (0, 2))
    text_in_grad, text_in_first, text_in_second, text_in_new, text_in_wn, text_in_rn = lamb_parts(text_inputs, first_text_inputs, second_text_inputs, weight_sums[1], (0, 2))
    head_out_grad, head_out_first, head_out_second, head_out_new, head_out_wn, head_out_rn = lamb_parts(head_outputs, first_head_outputs, second_head_outputs, weight_sums[2], (1, 2))
    mlp_in_grad, mlp_in_first, mlp_in_second, mlp_in_new, mlp_in_wn, mlp_in_rn = lamb_parts(mlp_inner, first_mlp_inner, second_mlp_inner, weight_sums[3], (0, 1))
    mlp_out_grad, mlp_out_first, mlp_out_second, mlp_out_new, mlp_out_wn, mlp_out_rn = lamb_parts(mlp_outer, first_mlp_outer, second_mlp_outer, weight_sums[4], (0, 1))
    skip_mat_grad, skip_mat_first, skip_mat_second, skip_mat_new, skip_mat_wn, skip_mat_rn = lamb_parts(skip_linear, first_skip_linear, second_skip_linear, weight_sums[5], (0, 1))
    shift_mat_grad, shift_mat_first, shift_mat_second, shift_mat_new, shift_mat_wn, shift_mat_rn = lamb_parts(shift_linear, first_shift_linear, second_shift_linear, weight_sums[6], (0, 1))
    row_gain_grad, row_gain_first, row_gain_second, row_gain_new, row_gain_wn, row_gain_rn = lamb_parts(row_gains, first_row_gains, second_row_gains, gain_sums[0], (1,))
    head_gain_grad, head_gain_first, head_gain_second, head_gain_new, head_gain_wn, head_gain_rn = lamb_parts(head_gains, first_head_gains, second_head_gains, gain_sums[1], (1,))
    weight_norms = jnp.concatenate([head_in_wn, text_in_wn, head_out_wn, mlp_in_wn, mlp_out_wn, skip_mat_wn, shift_mat_wn])
    ratio_norms = jnp.concatenate([head_in_rn, text_in_rn, head_out_rn, mlp_in_rn, mlp_out_rn, skip_mat_rn, shift_mat_rn])
    return (block_out, grad_latents, grad_skip_input, head_in_grad, head_in_first, head_in_second, head_in_new, text_in_grad, text_in_first, text_in_second, text_in_new, head_out_grad, head_out_first, head_out_second, head_out_new, mlp_in_grad, mlp_in_first, mlp_in_second, mlp_in_new, mlp_out_grad, mlp_out_first, mlp_out_second, mlp_out_new, skip_mat_grad, skip_mat_first, skip_mat_second, skip_mat_new, shift_mat_grad, shift_mat_first, shift_mat_second, shift_mat_new, row_gain_grad, row_gain_first, row_gain_second, row_gain_new, head_gain_grad, head_gain_first, head_gain_second, head_gain_new, weight_norms, ratio_norms)
```

```python
from functools import partial
import math

import jax
import jax.numpy as jnp
from jax import lax
from jax.sharding import PartitionSpec as P

D = 1408
HD = 88
GRID = 32


norm_eps = 1e-06
beta_one = 0.9
beta_two = 0.999
adam_eps = 1e-06
decay_rate = 0.01
learn_rate = 0.3
step_count = 10.0


def matmul(left, right):
    return jnp.dot(left, right, preferred_element_type=jnp.float32)


def matmul_tn(left, right):
    return lax.dot_general(
        left, right, (((0,), (0,)), ((), ())), preferred_element_type=jnp.float32
    )


def matmul_nt(left, right):
    return lax.dot_general(
        left, right, (((1,), (1,)), ((), ())), preferred_element_type=jnp.float32
    )


def norm_rows(values, factor):
    center = values - jnp.mean(values, axis=-1, keepdims=True)
    spread = jnp.mean(center * center, axis=-1, keepdims=True)
    return center * lax.rsqrt(spread + norm_eps) * factor


def rotate_pairs(values, cosines, sines):
    layout = values.shape
    paired = values.reshape(layout[:-1] + (layout[-1] // 2, 2))
    turned = jnp.stack([-paired[..., 1], paired[..., 0]], -1).reshape(layout)
    return values * cosines + turned * sines


def rotary_tables(patch_order):
    grid_row = (patch_order // GRID).astype(jnp.float32)
    grid_col = (patch_order % GRID).astype(jnp.float32)
    quarter = HD // 4
    spacing = 10000.0 ** (-jnp.arange(quarter).astype(jnp.float32) / quarter)
    row_angle = jnp.repeat(grid_row[:, None] * spacing[None, :], 2, axis=1)
    col_angle = jnp.repeat(grid_col[:, None] * spacing[None, :], 2, axis=1)
    angles = jnp.concatenate([row_angle, col_angle], 1)
    return (jnp.cos(angles)[:, None, :], jnp.sin(angles)[:, None, :])


def time_embed(timesteps):
    half_width = D // 2
    spacing = jnp.exp(-math.log(10000.0) * jnp.arange(half_width).astype(jnp.float32) / half_width)
    angles = timesteps.astype(jnp.float32)[:, None] * spacing[None, :]
    return jnp.concatenate([jnp.cos(angles), jnp.sin(angles)], -1)


def rope_heads(pre, factor, cosines, sines):
    return rotate_pairs(norm_rows(pre.reshape(pre.shape[0], -1, HD), factor), cosines, sines)


def plain_heads(pre, factor):
    return norm_rows(pre.reshape(pre.shape[0], -1, HD), factor)


def gelu_tanh(values):
    return jax.nn.gelu(values, approximate=True)


def attend(query, keys, values):
    factor = HD ** (-0.5)
    scores = jnp.einsum("qhd,khd->hqk", query, keys, preferred_element_type=jnp.float32) * factor
    highest = jnp.max(scores, axis=-1, keepdims=True)
    raised = jnp.exp(scores - highest)
    summed = jnp.sum(raised, axis=-1, keepdims=True)
    chances = raised / summed
    log_total = highest + jnp.log(summed)
    mixed = jnp.einsum(
        "hqk,khd->qhd", chances.astype(jnp.bfloat16), values, preferred_element_type=jnp.float32
    )
    return (mixed.astype(jnp.bfloat16), log_total)


def attend_back(query, keys, values, log_total, mixed_grad):
    factor = HD ** (-0.5)
    scores = jnp.einsum("qhd,khd->hqk", query, keys, preferred_element_type=jnp.float32) * factor
    chances = jnp.exp(scores - log_total)
    chance_grad = jnp.einsum("qhd,khd->hqk", mixed_grad, values, preferred_element_type=jnp.float32)
    centre = jnp.sum(chance_grad * chances, axis=-1, keepdims=True)
    score_grad = (chances * (chance_grad - centre)).astype(jnp.bfloat16)
    query_grad = (
        jnp.einsum("hqk,khd->qhd", score_grad, keys, preferred_element_type=jnp.float32) * factor
    )
    keys_grad = (
        jnp.einsum("hqk,qhd->khd", score_grad, query, preferred_element_type=jnp.float32) * factor
    )
    values_grad = jnp.einsum(
        "hqk,qhd->khd", chances.astype(jnp.bfloat16), mixed_grad, preferred_element_type=jnp.float32
    )
    return (query_grad, keys_grad, values_grad)


AXES = ("dp", "tensor")
BF16 = jnp.bfloat16
F32 = jnp.float32


def digits_of(count):
    found = []
    while count % 4 == 0:
        found.append(4)
        count //= 4
    if count > 1:
        found.append(count)
    return tuple(found)


def send(values, move):
    dp_count, tensor_count = lax.axis_size("dp"), lax.axis_size("tensor")
    pairs = []
    for d in range(dp_count):
        for t in range(tensor_count):
            d2, t2 = move(d, t)
            pairs.append((d * tensor_count + t, d2 * tensor_count + t2))
    return lax.ppermute(values, AXES, pairs)


def swap_core(values):
    return send(values, lambda d, t: (d, t ^ 1))


def swap_y(values):
    return send(values, lambda d, t: (d, t ^ 2))


class Digit:
    def __init__(self, sizes, at):
        self.size = sizes[at]
        self.stride = math.prod(sizes[at + 1 :])
        self.at = at
        self.mine = (lax.axis_index("dp") // self.stride) % self.size

    def step(self, values):
        def move(d, t):
            digit = (d // self.stride) % self.size
            return (d + ((digit + 1) % self.size - digit) * self.stride, t)

        return send(values, move)


def gather_digits(piece, digits, lead=0):
    done = []
    for digit in digits:
        axis = lead + sum(1 for other in done if other < digit.at)
        shape = piece.shape[:axis] + (digit.size,) + piece.shape[axis:]
        whole = jnp.zeros(shape, piece.dtype)
        for k in range(digit.size):
            if k:
                piece = digit.step(piece)
            place = (digit.mine - k) % digit.size
            whole = lax.dynamic_update_index_in_dim(whole, piece, place, axis)
        piece = whole
        done.append(digit.at)
    return piece


def add_low(left, right, dtype=BF16):
    return (left.astype(F32) + right.astype(F32)).astype(dtype)


def reduce_digits(parts, digits, lead=0, last=F32):
    left = sorted(digit.at for digit in digits)
    for at, digit in enumerate(digits):
        axis = lead + left.index(digit.at)
        left.remove(digit.at)

        def part(k):
            return lax.dynamic_index_in_dim(
                parts, (digit.mine - k) % digit.size, axis, keepdims=False
            )

        moving = part(1)
        for k in range(2, digit.size + 1):
            final = k == digit.size and at == len(digits) - 1
            moving = add_low(digit.step(moving), part(k), last if final else BF16)
        parts = moving
    return parts


def sum_everywhere(values, dp_only=False):
    bit = 1
    if not dp_only:
        while bit < lax.axis_size("tensor"):
            values = values + send(values, lambda d, t: (d, t ^ bit))
            bit *= 2
    bit = 1
    while bit < lax.axis_size("dp"):
        values = values + send(values, lambda d, t: (d ^ bit, t))
        bit *= 2
    return values


def gather_core(rows):
    return jnp.concatenate([rows, swap_core(rows)], 0)


def sum_core(rows):
    half = rows.shape[0] // 2
    return rows[:half] + swap_core(rows[half:].astype(BF16)).astype(F32)


def in_order(own, other, place, axis=0):
    first = jnp.where(place == 0, own, other)
    second = jnp.where(place == 0, other, own)
    return jnp.stack([first, second], axis)


def lamb_parts(master, first, second, grad):
    next_first = beta_one * first + (1.0 - beta_one) * grad
    next_second = beta_two * second + (1.0 - beta_two) * grad * grad
    ratio = (
        next_first
        / (1.0 - beta_one**step_count)
        / (jnp.sqrt(next_second / (1.0 - beta_two**step_count)) + adam_eps)
        + decay_rate * master
    )
    return (next_first, next_second, ratio)


def group_squares(values, axes):
    return jnp.sum(values * values, axis=axes).reshape(-1)


def row_renew(master, ratio):
    weight_norm = jnp.sqrt(jnp.sum(master * master, axis=1, keepdims=True))
    ratio_norm = jnp.sqrt(jnp.sum(ratio * ratio, axis=1, keepdims=True))
    return master - learn_rate * (weight_norm / ratio_norm) * ratio


def body(
    latents,
    skip_input,
    text_states,
    timesteps,
    patch_order,
    out_grad,
    head_inputs,
    first_head_inputs,
    second_head_inputs,
    text_inputs,
    first_text_inputs,
    second_text_inputs,
    head_outputs,
    first_head_outputs,
    second_head_outputs,
    mlp_inner,
    first_mlp_inner,
    second_mlp_inner,
    mlp_outer,
    first_mlp_outer,
    second_mlp_outer,
    skip_linear,
    first_skip_linear,
    second_skip_linear,
    shift_linear,
    first_shift_linear,
    second_shift_linear,
    row_gains,
    first_row_gains,
    second_row_gains,
    head_gains,
    first_head_gains,
    second_head_gains,
):
    dp_count = lax.axis_size("dp")
    tensor_count = lax.axis_size("tensor")
    me_d = lax.axis_index("dp")
    me_t = lax.axis_index("tensor")
    me_y = me_t // 2
    sizes = digits_of(dp_count)
    digits = [Digit(sizes, at) for at in range(len(sizes))]
    backwards = digits[::-1]
    width = latents.shape[2]
    block = latents.shape[1]
    rows = 2 * block
    depth = width // dp_count
    text_depth = text_inputs.shape[0]
    text_width = text_depth * dp_count
    head_cols = head_inputs.shape[2]
    hidden_cols = mlp_inner.shape[1]
    latent_count = 2 * dp_count

    low_head = head_inputs.astype(BF16)
    low_out = head_outputs.astype(BF16)
    half_depth = skip_linear.shape[0] // 2
    skip_half = lax.dynamic_slice_in_dim(skip_linear, (me_t % 2) * half_depth, half_depth, 0).astype(BF16)
    self_pack = jnp.concatenate([low_head[:, 0:3].reshape(depth, 3 * head_cols), low_out[0].T], 1)
    cross_pack = jnp.concatenate(
        [
            jnp.concatenate([low_head[:, 3], low_out[1].T], 1),
            text_inputs.astype(BF16).reshape(text_depth, 2 * head_cols),
        ],
        0,
    )
    mlp_pack = jnp.concatenate([mlp_inner.astype(BF16), mlp_outer.T.astype(BF16)], 1)

    def mine_first(pair):
        return (
            lax.dynamic_index_in_dim(pair, me_y, 0, keepdims=False),
            lax.dynamic_index_in_dim(pair, 1 - me_y, 0, keepdims=False),
        )

    def by_latent(own, other):
        return jnp.where(me_y == 0, jnp.stack([own, other]), jnp.stack([other, own]))

    joined_own, joined_other = mine_first(jnp.concatenate([latents, skip_input], -1))
    joined16 = jnp.concatenate([joined_own, swap_y(joined_other)], 0)
    skip_got = gather_digits(skip_half, digits)
    skip_pair = in_order(skip_got, swap_core(skip_got), me_t % 2, len(sizes))
    skip_mat = skip_pair.reshape(2 * width, width)
    self_near = gather_digits(self_pack, digits)
    self_near = self_near.reshape(width, 4 * head_cols)
    self_far = swap_y(self_near)
    cross_pair = gather_digits(jnp.stack([cross_pack, swap_y(cross_pack)]), digits, 1)
    cross_pair = cross_pair.reshape(2, dp_count, depth + text_depth, 2 * head_cols)
    mlp_got = gather_digits(mlp_pack, digits).reshape(width, 2 * hidden_cols)

    self_mats = [pack[:, : 3 * head_cols] for pack in (self_near, self_far)]
    self_outs = [pack[:, 3 * head_cols :] for pack in (self_near, self_far)]
    cross_mat = jnp.concatenate(
        [cross_pair[k, :, :depth, :head_cols].reshape(width, head_cols) for k in range(2)], 1
    )
    cross_out = jnp.concatenate(
        [cross_pair[k, :, :depth, head_cols:].reshape(width, head_cols) for k in range(2)], 1
    )
    text_mat = jnp.concatenate(
        [cross_pair[k, :, depth:, :head_cols].reshape(text_width, head_cols) for k in range(2)]
        + [cross_pair[k, :, depth:, head_cols:].reshape(text_width, head_cols) for k in range(2)],
        1,
    )
    self_out = jnp.concatenate(self_outs, 1)
    inner_mat, outer_mat = mlp_got[:, :hidden_cols], mlp_got[:, hidden_cols:]

    steps = jnp.zeros((dp_count, 2), F32)
    steps = lax.dynamic_update_slice(steps, timesteps.astype(F32)[None], (me_d, 0))
    steps = sum_everywhere(steps, dp_only=True).reshape(latent_count)
    silu16 = jax.nn.silu(time_embed(steps)).astype(BF16)
    silu_cols = lax.dynamic_slice_in_dim(silu16, me_d * depth, depth, 1)
    shifts = sum_everywhere(matmul(silu_cols, shift_linear.astype(BF16)), dp_only=True)
    my_latent = me_d * 2 + me_y
    shift = lax.dynamic_slice_in_dim(shifts, my_latent, 1, 0)

    places = patch_order.reshape(tensor_count, block)
    places = jnp.concatenate(
        [lax.dynamic_index_in_dim(places, me_t ^ k, 0, keepdims=False) for k in (0, 2, 1, 3)]
    )
    cosines, sines = rotary_tables(places)
    text_part = lax.dynamic_index_in_dim(text_states, me_y, 0, keepdims=False)

    cot_own, cot_other = mine_first(out_grad)
    cot_pair = jnp.concatenate([cot_own, cot_other], 0).astype(BF16)
    cot_got = swap_y(cot_pair)
    cotangent = jnp.concatenate([cot_own, cot_got[block:].astype(F32)], 0)
    mlp_full_grad = gather_core(
        jnp.concatenate([cot_pair[:block], cot_got[block:], cot_got[:block], cot_pair[block:]], 0)
    )

    skip_gain = row_gains[0:2].reshape(-1)
    normed, normed_back = jax.vjp(norm_rows, joined16.astype(F32), skip_gain)
    normed16 = normed.astype(BF16)
    hidden = matmul(normed16, skip_mat)
    first_norm, first_back = jax.vjp(norm_rows, hidden, row_gains[2])
    attn16 = (first_norm + shift).astype(BF16)
    attn_full = gather_core(attn16)
    self_pres = [matmul(attn_full, mat) for mat in self_mats]
    both = lambda k: jnp.concatenate(
        [pre[:, k * head_cols : (k + 1) * head_cols] for pre in self_pres], 1
    )
    rope = partial(rope_heads, cosines=cosines, sines=sines)
    query, query_back = jax.vjp(rope, both(0), head_gains[0])
    keys, keys_back = jax.vjp(rope, both(1), head_gains[1])
    query16, keys16 = query.astype(BF16), keys.astype(BF16)
    values16 = both(2).reshape(2 * rows, -1, HD).astype(BF16)
    self_out16, self_lse = attend(query16, keys16, values16)
    self_flat = self_out16.reshape(2 * rows, 2 * head_cols)
    after_self = hidden + sum_core(matmul_nt(self_flat, self_out))
    third_norm, third_back = jax.vjp(norm_rows, after_self, row_gains[3])
    cross_kept = gather_core(third_norm.astype(BF16))
    cross_query, cross_query_back = jax.vjp(rope, matmul(cross_kept, cross_mat), head_gains[2])
    text_pre = matmul(text_part, text_mat)
    text_keys, text_keys_back = jax.vjp(plain_heads, text_pre[:, : 2 * head_cols], head_gains[3])
    cross_query16, text_keys16 = cross_query.astype(BF16), text_keys.astype(BF16)
    text_rows = text_part.shape[0]
    text_values16 = text_pre[:, 2 * head_cols :].reshape(text_rows, -1, HD).astype(BF16)
    cross_out16, cross_lse = attend(cross_query16, text_keys16, text_values16)
    cross_flat = cross_out16.reshape(2 * rows, 2 * head_cols)
    after_cross = after_self + sum_core(matmul_nt(cross_flat, cross_out))
    second_norm, second_back = jax.vjp(norm_rows, after_cross, row_gains[4])

    mlp16 = second_norm.astype(BF16)
    mlp_kept = gather_core(jnp.concatenate([mlp16, swap_y(mlp16)], 0))
    inner = matmul(mlp_kept, inner_mat)
    activated, gelu_back = jax.vjp(gelu_tanh, inner)
    activated16 = activated.astype(BF16)

    def sum_chips(part):
        part = sum_core(part)
        return part[:rows] + swap_y(part[rows:].astype(BF16)).astype(F32)

    result = after_cross + sum_chips(matmul_nt(activated16, outer_mat))

    outer_wgrad = matmul_tn(mlp_full_grad, activated16)
    (inner_grad,) = gelu_back(matmul(mlp_full_grad, outer_mat))
    inner_grad16 = inner_grad.astype(BF16)
    inner_wgrad = matmul_tn(mlp_kept, inner_grad16)
    mlp_sum = jnp.concatenate([inner_wgrad.astype(BF16), outer_wgrad.astype(BF16)], 1)
    mlp_sum = reduce_digits(mlp_sum.reshape(*sizes, depth, 2 * hidden_cols), backwards)
    cross_res_grad, fifth_gain_grad = second_back(sum_chips(matmul_nt(inner_grad16, inner_mat)))
    after_cross_grad = cotangent + cross_res_grad
    cross_full_grad = gather_core(after_cross_grad.astype(BF16))
    cross_out_wgrad = matmul_tn(cross_full_grad, cross_flat).astype(BF16)
    cross_mixed_grad = matmul(cross_full_grad, cross_out).astype(BF16).reshape(2 * rows, -1, HD)
    cq_grad, ck_grad, cv_grad = attend_back(
        cross_query16, text_keys16, text_values16, cross_lse, cross_mixed_grad
    )
    cq_pre_grad, cq_gain_grad = cross_query_back(cq_grad)
    ck_pre_grad, ck_gain_grad = text_keys_back(ck_grad)
    text_grad16 = jnp.concatenate(
        [ck_pre_grad, cv_grad.reshape(text_rows, 2 * head_cols)], 1
    ).astype(BF16)
    text_wgrad = matmul_tn(text_part, text_grad16).astype(BF16)
    cq_pre16 = cq_pre_grad.astype(BF16)
    cross_q_wgrad = matmul_tn(cross_kept, cq_pre16).astype(BF16)
    cross_parts = []
    for k in range(2):
        near = slice(k * head_cols, (k + 1) * head_cols)
        far = slice((2 + k) * head_cols, (3 + k) * head_cols)
        top = jnp.concatenate([cross_q_wgrad[:, near], cross_out_wgrad[:, near]], 1)
        low = jnp.concatenate([text_wgrad[:, near], text_wgrad[:, far]], 1)
        top = top.reshape(*sizes, depth, 2 * head_cols)
        low = low.reshape(*sizes, text_depth, 2 * head_cols)
        cross_parts.append(jnp.concatenate([top, low], -2))
    cross_sum = reduce_digits(jnp.stack(cross_parts), backwards, 1, BF16)
    cross_sum = add_low(cross_sum[0], swap_y(cross_sum[1]), F32)
    self_res_grad, fourth_gain_grad = third_back(sum_core(matmul_nt(cq_pre16, cross_mat)))
    after_self_grad = after_cross_grad + self_res_grad
    self_full_grad = gather_core(after_self_grad.astype(BF16))
    self_out_wgrad = matmul_tn(self_full_grad, self_flat).astype(BF16)
    self_mixed_grad = matmul(self_full_grad, self_out).astype(BF16).reshape(2 * rows, -1, HD)
    sq_grad, sk_grad, sv_grad = attend_back(query16, keys16, values16, self_lse, self_mixed_grad)
    sq_pre_grad, sq_gain_grad = query_back(sq_grad)
    sk_pre_grad, sk_gain_grad = keys_back(sk_grad)
    pre_grads = [sq_pre_grad, sk_pre_grad, sv_grad.reshape(2 * rows, 2 * head_cols)]
    attn_part = 0.0
    self_parts = []
    for k in range(2):
        near = slice(k * head_cols, (k + 1) * head_cols)
        pre16 = jnp.concatenate([grad[:, near] for grad in pre_grads], 1).astype(BF16)
        attn_part = attn_part + matmul_nt(pre16, self_mats[k])
        in_wgrad = matmul_tn(attn_full, pre16).astype(BF16)
        part = jnp.concatenate([in_wgrad, self_out_wgrad[:, near]], 1)
        self_parts.append(part.reshape(*sizes, depth, 4 * head_cols))
    self_sum = add_low(self_parts[0], swap_y(self_parts[1]))
    self_sum = reduce_digits(self_sum, backwards)
    attn_grad = sum_core(attn_part)
    hidden_norm_grad, third_gain_grad = first_back(attn_grad)
    shift_grad = jnp.sum(attn_grad, axis=0)
    hidden_grad16 = (after_self_grad + hidden_norm_grad).astype(BF16)
    skip_wgrad = matmul_tn(normed16, hidden_grad16).astype(BF16)
    joined_grad, skip_gain_grad = normed_back(matmul_nt(hidden_grad16, skip_mat))

    quarter = half_depth // 2
    skip_parts = skip_wgrad.reshape(dp_count, 2, 2, quarter, width)
    mine = lax.dynamic_index_in_dim(skip_parts, me_t % 2, 2, keepdims=False)
    theirs = lax.dynamic_index_in_dim(skip_parts, 1 - me_t % 2, 2, keepdims=False)
    skip_parts = add_low(mine, swap_core(theirs))
    mine = lax.dynamic_index_in_dim(skip_parts, me_y, 1, keepdims=False)
    theirs = lax.dynamic_index_in_dim(skip_parts, 1 - me_y, 1, keepdims=False)
    skip_parts = add_low(mine, swap_y(theirs)).reshape(*sizes, quarter, width)
    skip_sum = reduce_digits(skip_parts, backwards, 0, BF16)
    skip_pair = in_order(skip_sum, swap_core(skip_sum), me_t % 2)
    skip_all = in_order(skip_pair, swap_y(skip_pair), me_y)
    skip_mat_grad = skip_all.reshape(2 * half_depth, width).astype(F32)

    row_grad = jnp.stack(
        [
            skip_gain_grad[:width],
            skip_gain_grad[width:],
            third_gain_grad,
            fourth_gain_grad,
            fifth_gain_grad,
        ]
    )
    head_grad = jnp.stack([sq_gain_grad, sk_gain_grad, cq_gain_grad, ck_gain_grad])
    single = jnp.zeros((latent_count, width), F32)
    single = lax.dynamic_update_slice(single, shift_grad[None], (my_latent, 0))
    head_row = jnp.pad(head_grad.reshape(1, -1), ((0, 0), (0, width - head_grad.size)))
    single = sum_everywhere(jnp.concatenate([single, row_grad, head_row], 0))
    row_gain_grad = single[latent_count : latent_count + 5]
    head_gain_grad = single[latent_count + 5, : head_grad.size].reshape(head_grad.shape)
    shift_mat_grad = lax.dot_general(
        silu_cols.astype(F32),
        single[:latent_count],
        (((0,), (0,)), ((), ())),
        precision=lax.Precision.HIGHEST,
        preferred_element_type=F32,
    )

    head_in_grad = jnp.concatenate(
        [
            self_sum[:, : 3 * head_cols].reshape(depth, 3, head_cols),
            cross_sum[:depth, None, :head_cols],
        ],
        1,
    )
    text_in_grad = cross_sum[depth:].reshape(text_depth, 2, head_cols)
    head_out_grad = jnp.stack([self_sum[:, 3 * head_cols :].T, cross_sum[:depth, head_cols:].T])
    mlp_in_grad = mlp_sum[:, :hidden_cols]
    mlp_out_grad = mlp_sum[:, hidden_cols:].T

    def put_back(values):
        return by_latent(values[:block], swap_y(values[block:].astype(BF16)).astype(F32))

    block_out = put_back(result)
    grad_latents = put_back(joined_grad[:, :width])
    grad_skip_input = put_back(joined_grad[:, width:])
    head_in_first, head_in_second, head_in_ratio = lamb_parts(
        head_inputs, first_head_inputs, second_head_inputs, head_in_grad
    )
    text_in_first, text_in_second, text_in_ratio = lamb_parts(
        text_inputs, first_text_inputs, second_text_inputs, text_in_grad
    )
    head_out_first, head_out_second, head_out_ratio = lamb_parts(
        head_outputs, first_head_outputs, second_head_outputs, head_out_grad
    )
    mlp_in_first, mlp_in_second, mlp_in_ratio = lamb_parts(
        mlp_inner, first_mlp_inner, second_mlp_inner, mlp_in_grad
    )
    mlp_out_first, mlp_out_second, mlp_out_ratio = lamb_parts(
        mlp_outer, first_mlp_outer, second_mlp_outer, mlp_out_grad
    )
    skip_mat_first, skip_mat_second, skip_mat_ratio = lamb_parts(
        skip_linear, first_skip_linear, second_skip_linear, skip_mat_grad
    )
    shift_mat_first, shift_mat_second, shift_mat_ratio = lamb_parts(
        shift_linear, first_shift_linear, second_shift_linear, shift_mat_grad
    )
    weight_squares = jnp.concatenate(
        [
            group_squares(head_inputs, (0, 2)),
            group_squares(text_inputs, (0, 2)),
            group_squares(head_outputs, (1, 2)),
            group_squares(mlp_inner, (0, 1)),
            group_squares(mlp_outer, (0, 1)),
            group_squares(skip_linear, (0, 1)),
            group_squares(shift_linear, (0, 1)),
        ]
    )
    ratio_squares = jnp.concatenate(
        [
            group_squares(head_in_ratio, (0, 2)),
            group_squares(text_in_ratio, (0, 2)),
            group_squares(head_out_ratio, (1, 2)),
            group_squares(mlp_in_ratio, (0, 1)),
            group_squares(mlp_out_ratio, (0, 1)),
            group_squares(skip_mat_ratio, (0, 1)),
            group_squares(shift_mat_ratio, (0, 1)),
        ]
    )
    weight_squares, ratio_squares = sum_everywhere(jnp.stack([weight_squares, ratio_squares]))
    correction = jnp.concatenate(
        [jnp.ones((10,), jnp.float32), jnp.full((2,), 1.0 / lax.axis_size("tensor"), jnp.float32)]
    )
    weight_norms = jnp.sqrt(weight_squares * correction)
    ratio_norms = jnp.sqrt(ratio_squares * correction)
    trust = weight_norms / ratio_norms
    head_in_new = head_inputs - learn_rate * trust[0:4][None, :, None] * head_in_ratio
    text_in_new = text_inputs - learn_rate * trust[4:6][None, :, None] * text_in_ratio
    head_out_new = head_outputs - learn_rate * trust[6:8][:, None, None] * head_out_ratio
    mlp_in_new = mlp_inner - learn_rate * trust[8] * mlp_in_ratio
    mlp_out_new = mlp_outer - learn_rate * trust[9] * mlp_out_ratio
    skip_mat_new = skip_linear - learn_rate * trust[10] * skip_mat_ratio
    shift_mat_new = shift_linear - learn_rate * trust[11] * shift_mat_ratio
    row_gain_first, row_gain_second, row_gain_ratio = lamb_parts(
        row_gains, first_row_gains, second_row_gains, row_gain_grad
    )
    head_gain_first, head_gain_second, head_gain_ratio = lamb_parts(
        head_gains, first_head_gains, second_head_gains, head_gain_grad
    )
    row_gain_new = row_renew(row_gains, row_gain_ratio)
    head_gain_new = row_renew(head_gains, head_gain_ratio)
    return (
        block_out,
        grad_latents,
        grad_skip_input,
        head_in_grad,
        head_in_first,
        head_in_second,
        head_in_new,
        text_in_grad,
        text_in_first,
        text_in_second,
        text_in_new,
        head_out_grad,
        head_out_first,
        head_out_second,
        head_out_new,
        mlp_in_grad,
        mlp_in_first,
        mlp_in_second,
        mlp_in_new,
        mlp_out_grad,
        mlp_out_first,
        mlp_out_second,
        mlp_out_new,
        skip_mat_grad,
        skip_mat_first,
        skip_mat_second,
        skip_mat_new,
        shift_mat_grad,
        shift_mat_first,
        shift_mat_second,
        shift_mat_new,
        row_gain_grad,
        row_gain_first,
        row_gain_second,
        row_gain_new,
        head_gain_grad,
        head_gain_first,
        head_gain_second,
        head_gain_new,
        weight_norms,
        ratio_norms,
    )


def solution(mesh):
    return jax.shard_map(
        body,
        mesh=mesh,
        in_specs=(
            P("dp", "tensor", None),
            P("dp", "tensor", None),
            P("dp", None, None),
            P("dp"),
            P(),
            P("dp", "tensor", None),
            P("dp", None, "tensor"),
            P("dp", None, "tensor"),
            P("dp", None, "tensor"),
            P("dp", None, "tensor"),
            P("dp", None, "tensor"),
            P("dp", None, "tensor"),
            P(None, "tensor", "dp"),
            P(None, "tensor", "dp"),
            P(None, "tensor", "dp"),
            P("dp", "tensor"),
            P("dp", "tensor"),
            P("dp", "tensor"),
            P("tensor", "dp"),
            P("tensor", "dp"),
            P("tensor", "dp"),
            P("dp", None),
            P("dp", None),
            P("dp", None),
            P("dp", None),
            P("dp", None),
            P("dp", None),
            P(),
            P(),
            P(),
            P(),
            P(),
            P(),
        ),
        out_specs=(
            P("dp", "tensor", None),
            P("dp", "tensor", None),
            P("dp", "tensor", None),
            P("dp", None, "tensor"),
            P("dp", None, "tensor"),
            P("dp", None, "tensor"),
            P("dp", None, "tensor"),
            P("dp", None, "tensor"),
            P("dp", None, "tensor"),
            P("dp", None, "tensor"),
            P("dp", None, "tensor"),
            P(None, "tensor", "dp"),
            P(None, "tensor", "dp"),
            P(None, "tensor", "dp"),
            P(None, "tensor", "dp"),
            P("dp", "tensor"),
            P("dp", "tensor"),
            P("dp", "tensor"),
            P("dp", "tensor"),
            P("tensor", "dp"),
            P("tensor", "dp"),
            P("tensor", "dp"),
            P("tensor", "dp"),
            P("dp", None),
            P("dp", None),
            P("dp", None),
            P("dp", None),
            P("dp", None),
            P("dp", None),
            P("dp", None),
            P("dp", None),
            P(),
            P(),
            P(),
            P(),
            P(),
            P(),
            P(),
            P(),
            P(),
            P(),
        ),
        check_vma=False,
    )
```

```python
from functools import partial
import itertools
import math

import jax
import jax.numpy as jnp
from jax import lax
from jax.experimental import pallas as pl
from jax.experimental.pallas import tpu as pltpu
from jax.sharding import PartitionSpec as P

D = 1408
HD = 88
GRID = 32


norm_eps = 1e-06
beta_one = 0.9
beta_two = 0.999
adam_eps = 1e-06
decay_rate = 0.01
learn_rate = 0.3
step_count = 10.0

BF16 = jnp.bfloat16
F32 = jnp.float32


def matmul(left, right):
    return jnp.dot(left, right, preferred_element_type=jnp.float32)


def matmul_tn(left, right):
    return lax.dot_general(
        left, right, (((0,), (0,)), ((), ())), preferred_element_type=jnp.float32
    )


def matmul_nt(left, right):
    return lax.dot_general(
        left, right, (((1,), (1,)), ((), ())), preferred_element_type=jnp.float32
    )


def norm_rows(values, factor):
    center = values - jnp.mean(values, axis=-1, keepdims=True)
    spread = jnp.mean(center * center, axis=-1, keepdims=True)
    return center * lax.rsqrt(spread + norm_eps) * factor


def rotary_tables(places):
    grid_row = (places // GRID).astype(jnp.float32)
    grid_col = (places % GRID).astype(jnp.float32)
    quarter = HD // 4
    spacing = 10000.0 ** (-jnp.arange(quarter).astype(jnp.float32) / quarter)
    row_angle = jnp.repeat(grid_row[:, None] * spacing[None, :], 2, axis=1)
    col_angle = jnp.repeat(grid_col[:, None] * spacing[None, :], 2, axis=1)
    angles = jnp.concatenate([row_angle, col_angle], 1)
    even = jnp.arange(HD) % 2 == 0
    sines = jnp.sin(angles)
    tables = (jnp.cos(angles), jnp.where(even, -sines, 0.0), jnp.where(even, 0.0, sines))
    return tuple(jnp.pad(table, ((0, 0), (0, LANES - HD))) for table in tables)


def time_embed(timesteps):
    half_width = D // 2
    spacing = jnp.exp(-math.log(10000.0) * jnp.arange(half_width).astype(jnp.float32) / half_width)
    angles = timesteps.astype(jnp.float32)[:, None] * spacing[None, :]
    return jnp.concatenate([jnp.cos(angles), jnp.sin(angles)], -1)


def gelu_tanh(values):
    return jax.nn.gelu(values, approximate=True)


LANES = 128
Q_SCALE = math.log2(math.e) * HD**-0.5
FAR = -10000.0


def head_slice(ref, at):
    width = ref.shape[1]
    if at + LANES <= width:
        values = ref[:, at : at + LANES]
    else:
        values = pltpu.roll(ref[:, width - LANES :], width - at, 1)
    return jnp.where(lanes_of(values) < HD, values, 0.0)


def lanes_of(values):
    return lax.broadcasted_iota(jnp.int32, values.shape, 1)


def head_norm(pre):
    mean = jnp.sum(pre, axis=1, keepdims=True) * (1.0 / HD)
    center = jnp.where(lanes_of(pre) < HD, pre - mean, 0.0)
    spread = jnp.sum(center * center, axis=1, keepdims=True) * (1.0 / HD)
    scale = lax.rsqrt(spread + norm_eps)
    return center * scale, scale


def turn(values, tables):
    cosines, after, before = (table[...] for table in tables)
    return (
        values * cosines
        + pltpu.roll(values, LANES - 1, 1) * after
        + pltpu.roll(values, 1, 1) * before
    )


def turn_back(grads, tables):
    cosines, after, before = (table[...] for table in tables)
    return (
        grads * cosines
        + pltpu.roll(grads * after, 1, 1)
        + pltpu.roll(grads * before, LANES - 1, 1)
    )


def head_norm_back(grads, gain, normed, scale):
    gain_grad = jnp.sum(grads * normed, axis=0, keepdims=True)
    grads = grads * gain
    mean = jnp.sum(grads, axis=1, keepdims=True) * (1.0 / HD)
    along = jnp.sum(grads * normed, axis=1, keepdims=True) * (1.0 / HD)
    back = scale * (grads - mean - normed * along)
    return jnp.where(lanes_of(back) < HD, back, 0.0), gain_grad


def dot_nt(left, right):
    return lax.dot_general(left, right, (((1,), (1,)), ((), ())), preferred_element_type=F32)


def with_pair(values, column, lanes):
    high = column.astype(BF16).astype(F32)
    return jnp.where(lanes == HD, high, jnp.where(lanes == HD + 1, column - high, values))


def attend_kernel(heads, q_at, k_at, v_at, one_pre, key_rows, *refs):
    if one_pre:
        refs = (refs[0],) + refs
    q_ref, kv_ref, gain_ref, cos_ref, after_ref, before_ref = refs[:6]
    out_ref, q_ext_ref, k_ext_ref, v_ext_ref, flat_ref = refs[6:]
    tables = (cos_ref, after_ref, before_ref)
    rows, keys_count = q_ref.shape[0], kv_ref.shape[0]
    step = min(rows, 256)
    for h in range(heads):
        ext = slice(h * LANES, (h + 1) * LANES)
        normed, _ = head_norm(head_slice(q_ref, q_at + h * HD))
        lanes = lanes_of(normed)
        query = turn(normed * gain_ref[0:1], tables) * Q_SCALE
        query = jnp.where(lanes == HD + 2, FAR, query)
        q_ext_ref[:, ext] = query.astype(BF16)
        normed, _ = head_norm(head_slice(kv_ref, k_at + h * HD))
        keys = normed * gain_ref[1:2]
        if one_pre:
            keys = turn(keys, tables)
        lanes = lanes_of(keys)
        keys = jnp.where((lanes == HD) | (lanes == HD + 1), 1.0, keys)
        if key_rows < keys_count:
            places = lax.broadcasted_iota(jnp.int32, keys.shape, 0)
            keys = jnp.where((lanes == HD + 2) & (places >= key_rows), 1.0, keys)
        keys16 = keys.astype(BF16)
        k_ext_ref[:, ext] = keys16
        values = head_slice(kv_ref, v_at + h * HD)
        values16 = jnp.where((lanes == HD) | (lanes == HD + 1), 1.0, values).astype(BF16)
        v_ext_ref[:, ext] = values16
        for at in range(0, rows, step):
            part = slice(at, at + step)
            query16 = q_ext_ref[part, ext]
            raised = jnp.exp2(dot_nt(query16, keys16)).astype(BF16)
            mixed = jnp.dot(raised, values16, preferred_element_type=F32)
            total = mixed[:, HD : HD + 1]
            mixed = mixed * (1.0 / total)
            flat_ref[part, h * HD : (h + 1) * HD] = mixed[:, :HD]
            query = query16.astype(F32)
            query = with_pair(query, -jnp.log2(total), lanes_of(query))
            q_ext_ref[part, ext] = query.astype(BF16)
    out_ref[...] = flat_ref[...].astype(BF16)


def attend_back_kernel(heads, q_at, k_at, v_at, one_pre, *refs):
    if one_pre:
        refs = (refs[0],) + refs
    q_ref, kv_ref, gain_ref, cos_ref, after_ref, before_ref = refs[:6]
    out_ref, grad_ref, q_ext_ref, k_ext_ref, v_ext_ref = refs[6:11]
    if one_pre:
        pre_grad_ref, gain_grad_ref, flat_ref, out_flat, grad_flat = refs[11:]
        q_flat = kv_flat = flat_ref
    else:
        q_grad_ref, kv_grad_ref, gain_grad_ref, q_flat, kv_flat, out_flat, grad_flat = refs[11:]
    tables = (cos_ref, after_ref, before_ref)
    rows, keys_count = q_ref.shape[0], kv_ref.shape[0]
    step = 256 if keys_count % 256 == 0 else keys_count
    out_flat[...] = out_ref[...].astype(F32)
    grad_flat[...] = grad_ref[...].astype(F32)
    q_gain = jnp.zeros((1, LANES), F32)
    k_gain = jnp.zeros((1, LANES), F32)
    for h in range(heads):
        ext = slice(h * LANES, (h + 1) * LANES)
        grad = head_slice(grad_flat, h * HD)
        delta = jnp.sum(grad * head_slice(out_flat, h * HD), axis=1, keepdims=True)
        grad16 = with_pair(grad, -delta, lanes_of(grad)).astype(BF16)
        query16 = q_ext_ref[:, ext]
        query_grad = jnp.zeros((LANES, rows), F32)
        keys_grad = []
        for at in range(0, keys_count, step):
            part = slice(at, at + step)
            keys16, values16 = k_ext_ref[part, ext], v_ext_ref[part, ext]
            chances = jnp.exp2(dot_nt(keys16, query16))
            score_grad = (chances * dot_nt(values16, grad16)).astype(BF16)
            value_grad = jnp.dot(chances.astype(BF16), grad16, preferred_element_type=F32)
            kv_flat[part, v_at + h * HD : v_at + (h + 1) * HD] = value_grad[:, :HD]
            keys_grad.append(jnp.dot(score_grad, query16, preferred_element_type=F32))
            query_grad = query_grad + lax.dot_general(
                keys16, score_grad, (((0,), (0,)), ((), ())), preferred_element_type=F32
            )
        query_grad = query_grad.T * (HD**-0.5)
        normed, scale = head_norm(head_slice(q_ref, q_at + h * HD))
        query_grad = jnp.where(lanes_of(query_grad) < HD, query_grad, 0.0)
        back, gain_grad = head_norm_back(turn_back(query_grad, tables), gain_ref[0:1], normed, scale)
        q_gain = q_gain + gain_grad
        q_flat[:, q_at + h * HD : q_at + (h + 1) * HD] = back[:, :HD]
        key_grad = jnp.concatenate(keys_grad, 0) * math.log(2.0)
        key_grad = jnp.where(lanes_of(key_grad) < HD, key_grad, 0.0)
        if one_pre:
            key_grad = turn_back(key_grad, tables)
        normed, scale = head_norm(head_slice(kv_ref, k_at + h * HD))
        back, gain_grad = head_norm_back(key_grad, gain_ref[1:2], normed, scale)
        k_gain = k_gain + gain_grad
        kv_flat[:, k_at + h * HD : k_at + (h + 1) * HD] = back[:, :HD]
    gain_grad_ref[...] = jnp.concatenate([q_gain, k_gain, jnp.zeros((6, LANES), F32)], 0)
    if one_pre:
        pre_grad_ref[...] = flat_ref[...].astype(BF16)
    else:
        q_grad_ref[...] = q_flat[...].astype(BF16)
        kv_grad_ref[...] = kv_flat[...].astype(BF16)


VMEM_LIMIT = 60 * 1024 * 1024


def attend(pres, gains, tables, heads, places, key_rows):
    rows, keys_count = pres[0].shape[0], pres[-1].shape[0]
    return pl.pallas_call(
        partial(attend_kernel, heads, *places, len(pres) == 1, key_rows),
        out_shape=(
            jax.ShapeDtypeStruct((rows, heads * HD), BF16),
            jax.ShapeDtypeStruct((rows, heads * LANES), BF16),
            jax.ShapeDtypeStruct((keys_count, heads * LANES), BF16),
            jax.ShapeDtypeStruct((keys_count, heads * LANES), BF16),
        ),
        scratch_shapes=[pltpu.VMEM((rows, heads * HD), F32)],
        compiler_params=pltpu.CompilerParams(vmem_limit_bytes=VMEM_LIMIT),
        cost_estimate=pl.CostEstimate(flops=0, bytes_accessed=0, transcendentals=0),
    )(*pres, gains, *tables)


def attend_back(pres, gains, tables, kept, out_grad, heads, places):
    rows, keys_count = pres[0].shape[0], pres[-1].shape[0]
    return pl.pallas_call(
        partial(attend_back_kernel, heads, *places, len(pres) == 1),
        out_shape=tuple(jax.ShapeDtypeStruct(pre.shape, BF16) for pre in pres)
        + (jax.ShapeDtypeStruct((8, LANES), F32),),
        scratch_shapes=[pltpu.VMEM(pre.shape, F32) for pre in pres]
        + [pltpu.VMEM((rows, heads * HD), F32)] * 2,
        compiler_params=pltpu.CompilerParams(vmem_limit_bytes=VMEM_LIMIT),
        cost_estimate=pl.CostEstimate(flops=0, bytes_accessed=0, transcendentals=0),
    )(*pres, gains, *tables, kept[0], out_grad, *kept[1:])


AXES = ("dp", "tensor")


def digits_of(count):
    found = []
    while count % 4 == 0:
        found.append(4)
        count //= 4
    if count > 1:
        found.append(count)
    return tuple(found)


def send(values, move):
    dp_count, tensor_count = lax.axis_size("dp"), lax.axis_size("tensor")
    pairs = []
    for d in range(dp_count):
        for t in range(tensor_count):
            d2, t2 = move(d, t)
            pairs.append((d * tensor_count + t, d2 * tensor_count + t2))
    return lax.ppermute(values, AXES, pairs)


def swap_core(values):
    return send(values, lambda d, t: (d, t ^ 1))


def swap_y(values):
    return send(values, lambda d, t: (d, t ^ 2))


def after(values, *others):
    return lax.optimization_barrier((values, others))[0]


def plan(sizes):
    nodes = list(itertools.product(*map(range, sizes)))
    have, left, steps = {nodes[0]}, nodes[1:], []

    def ways(node):
        return [ring for ring in range(len(sizes)) if node[ring] and before(node, ring) in have]

    while left:
        step, taken = [], set()
        for ring in range(len(sizes)):
            ready = [node for node in left if node not in taken and ring in ways(node)]
            if ready:
                node = min(ready, key=lambda n: (len(ways(n)), -n[0] if ring == 0 else n[0], n))
                step.append((ring, node))
                taken.add(node)
        have |= taken
        left = [node for node in left if node not in taken]
        steps.append(step)
    return steps


def before(node, ring):
    return node[:ring] + (node[ring] - 1,) + node[ring + 1 :]


class Grid:
    def __init__(self, sizes, with_y):
        self.sizes = sizes
        self.with_y = with_y
        self.strides = [math.prod(sizes[at + 1 :]) for at in range(len(sizes))]
        me = lax.axis_index("dp")
        self.mine = [(me // stride) % size for size, stride in zip(sizes, self.strides)]
        self.steps = plan(sizes + ((2,) if with_y else ()))
        self.nodes = list(itertools.product(*map(range, sizes + ((2,) if with_y else ()))))

    def shift(self, values, ring, by):
        if ring == len(self.sizes):
            return swap_y(values)
        size, stride = self.sizes[ring], self.strides[ring]

        def move(d, t):
            digit = (d // stride) % size
            return (d + ((digit + by) % size - digit) * stride, t)

        return send(values, move)

    def owner(self, node):
        return sum(
            ((mine - far) % size) * stride
            for mine, far, size, stride in zip(self.mine, node, self.sizes, self.strides)
        )


def place_kernel(count, axis, spots_ref, *refs):
    sources, (out_ref, held_ref, in_sems, out_sems) = refs[:count], refs[count:]
    before_axis = (slice(None),) * axis
    reads = [
        pltpu.make_async_copy(source, held_ref.at[k], in_sems.at[k])
        for k, source in enumerate(sources)
    ]
    writes = [
        pltpu.make_async_copy(held_ref.at[k], out_ref.at[before_axis + (spots_ref[k],)], out_sems.at[k])
        for k in range(count)
    ]
    for read in reads:
        read.start()
    for read, write in zip(reads, writes):
        read.wait()
        write.start()
    for write in writes:
        write.wait()


def place(pieces, spots, axis=0):
    count = len(pieces)
    shape = pieces[0].shape
    return pl.pallas_call(
        partial(place_kernel, count, axis),
        out_shape=jax.ShapeDtypeStruct(shape[:axis] + (count,) + shape[axis:], pieces[0].dtype),
        in_specs=[pl.BlockSpec(memory_space=pltpu.SMEM)]
        + [pl.BlockSpec(memory_space=pl.ANY)] * count,
        out_specs=pl.BlockSpec(memory_space=pl.ANY),
        scratch_shapes=[
            pltpu.VMEM((count,) + pieces[0].shape, pieces[0].dtype),
            pltpu.SemaphoreType.DMA((count,)),
            pltpu.SemaphoreType.DMA((count,)),
        ],
        compiler_params=pltpu.CompilerParams(vmem_limit_bytes=VMEM_LIMIT),
        cost_estimate=pl.CostEstimate(flops=0, bytes_accessed=0, transcendentals=0),
    )(jnp.stack([jnp.asarray(spot, jnp.int32) for spot in spots]), *pieces)


class Fetch:
    def __init__(self, grid, piece):
        self.grid = grid
        self.got = {grid.nodes[0]: piece}
        self.small = math.prod(grid.sizes) <= 8
        self.todo = list(grid.steps) if self.small else []

    def advance(self, *waits):
        new = {}
        if self.todo:
            for ring, node in self.todo.pop(0):
                source = self.got[before(node, ring)]
                source = after(source, *waits) if waits else source
                new[node] = self.grid.shift(source, ring, 1)
        self.got.update(new)
        return tuple(new.values())

    def finish(self):
        grid, piece = self.grid, self.got[self.grid.nodes[0]]
        if not self.small:
            whole = lax.all_gather(piece, "dp")
            return jnp.stack([whole, swap_y(whole)]) if grid.with_y else whole
        count = math.prod(grid.sizes)
        spots = [grid.owner(node) + (node[-1] * count if grid.with_y else 0) for node in grid.nodes]
        whole = place([self.got[node] for node in grid.nodes], spots)
        return whole.reshape((2, count) + piece.shape) if grid.with_y else whole


class Sequence:
    def __init__(self):
        self.came = ()

    def run(self, *jobs, since=()):
        waits = self.came + tuple(since)
        self.came = tuple(got for job in jobs for got in job.advance(*waits))
        return self.came


class Reduction:
    def __init__(self, grid, part, last=F32):
        self.grid, self.part, self.last = grid, part, last
        self.small = math.prod(grid.sizes) <= 8
        self.sums = {node: [] for node in grid.nodes}
        self.todo = list(reversed(grid.steps)) if self.small else []

    def total(self, node, dtype):
        dp_index = self.grid.owner(node)
        value = self.part(dp_index, node[-1] if self.grid.with_y else 0).astype(F32)
        for got in self.sums[node]:
            value = value + got.astype(F32)
        return value.astype(dtype)

    def advance(self, *waits):
        came = []
        if self.todo:
            for ring, node in self.todo.pop(0):
                moving = self.total(node, BF16)
                moving = after(moving, *waits) if waits else moving
                got = self.grid.shift(moving, ring, -1)
                self.sums[before(node, ring)].append(got)
                came.append(got)
        return came

    def finish(self):
        while self.todo:
            self.advance()
        if self.small:
            return self.total(self.grid.nodes[0], self.last)
        count = math.prod(self.grid.sizes)
        blocks = []
        for far in range(2 if self.grid.with_y else 1):
            whole = jnp.stack([self.part(k, far) for k in range(count)]).astype(F32)
            whole = lax.psum_scatter(whole, "dp", scatter_dimension=0, tiled=False)
            blocks.append(whole)
        if self.grid.with_y:
            return (blocks[0] + swap_y(blocks[1].astype(BF16)).astype(F32)).astype(self.last)
        return blocks[0].astype(self.last)


def mlp_kernel(half_steps, x_ref, grad_ref, mats_ref, act_ref, inner_grad_ref, *part_refs):
    hidden = act_ref.shape[1]
    inner_mat, outer_mat = mats_ref[:, :hidden], mats_ref[:, hidden:]
    inner = jnp.dot(x_ref[...], inner_mat, preferred_element_type=F32)
    grad = jnp.dot(grad_ref[...], outer_mat, preferred_element_type=F32)
    square = inner * inner
    bend = math.sqrt(2.0 / math.pi)
    turned = jnp.tanh(inner * (bend + (bend * 0.044715) * square))
    rise = 0.5 + 0.5 * turned
    slope = rise + (0.5 * inner) * (1.0 - turned * turned) * (bend + (bend * 3 * 0.044715) * square)
    act_ref[...] = (inner * rise).astype(BF16)
    inner_grad_ref[...] = (grad * slope).astype(BF16)
    out = dot_nt(act_ref[...], outer_mat).astype(BF16)
    in_grad = dot_nt(inner_grad_ref[...], inner_mat).astype(BF16)
    first = pl.program_id(0) < half_steps

    @pl.when(first)
    def _():
        part_refs[0][...] = out
        part_refs[1][...] = in_grad

    @pl.when(jnp.logical_not(first))
    def _():
        part_refs[2][...] = out
        part_refs[3][...] = in_grad


def mlp_both(tokens, grads, mats):
    count, width = tokens.shape
    hidden = mats.shape[1] // 2
    block = 256
    steps = count // block
    half = steps // 2
    row = lambda i: (i, 0)
    mine = lambda i: (jnp.minimum(i, half - 1), 0)
    theirs = lambda i: (jnp.maximum(i - half, 0), 0)
    share = jax.ShapeDtypeStruct((count // 2, width), BF16)
    return pl.pallas_call(
        partial(mlp_kernel, half),
        grid=(steps,),
        in_specs=[
            pl.BlockSpec((block, width), row),
            pl.BlockSpec((block, width), row),
            pl.BlockSpec((width, 2 * hidden), lambda i: (0, 0)),
        ],
        out_specs=[pl.BlockSpec((block, hidden), row)] * 2
        + [pl.BlockSpec((block, width), mine)] * 2
        + [pl.BlockSpec((block, width), theirs)] * 2,
        out_shape=[jax.ShapeDtypeStruct((count, hidden), BF16)] * 2 + [share] * 4,
        compiler_params=pltpu.CompilerParams(vmem_limit_bytes=VMEM_LIMIT),
        cost_estimate=pl.CostEstimate(flops=0, bytes_accessed=0, transcendentals=0),
    )(tokens, grads, mats)


def wgrad_kernel(left_ref, right_ref, out_ref, turned_ref):
    @pl.when(pl.program_id(0) == 0)
    def _():
        for at in range(0, left_ref.shape[1], LANES):
            turned_ref[at : at + LANES] = left_ref[:, at : at + LANES].T

    out_ref[...] = jnp.dot(turned_ref[...], right_ref[...], preferred_element_type=F32).astype(BF16)


def wgrad(left, right):
    (count, rows), columns = left.shape, right.shape[1]
    block = 512 if columns % 512 == 0 else columns
    return pl.pallas_call(
        wgrad_kernel,
        grid=(columns // block,),
        in_specs=[
            pl.BlockSpec((count, rows), lambda i: (0, 0)),
            pl.BlockSpec((count, block), lambda i: (0, i)),
        ],
        out_specs=pl.BlockSpec((rows, block), lambda i: (0, i)),
        out_shape=jax.ShapeDtypeStruct((rows, columns), BF16),
        scratch_shapes=[pltpu.VMEM((rows, count), BF16)],
        compiler_params=pltpu.CompilerParams(vmem_limit_bytes=VMEM_LIMIT),
        cost_estimate=pl.CostEstimate(flops=0, bytes_accessed=0, transcendentals=0),
    )(left, right)


def add_low(left, right, dtype=BF16):
    return (left.astype(F32) + right.astype(F32)).astype(dtype)


def sum_everywhere(values, dp_only=False):
    bit = 1
    if not dp_only:
        while bit < lax.axis_size("tensor"):
            values = values + send(values, lambda d, t: (d, t ^ bit))
            bit *= 2
    bit = 1
    while bit < lax.axis_size("dp"):
        values = values + send(values, lambda d, t: (d ^ bit, t))
        bit *= 2
    return values


def gather_core(rows):
    return jnp.concatenate([rows, swap_core(rows)], 0)


def sum_core(rows):
    half = rows.shape[0] // 2
    return rows[:half] + swap_core(rows[half:].astype(BF16)).astype(F32)


def in_order(own, other, place, axis=0):
    first = jnp.where(place == 0, own, other)
    second = jnp.where(place == 0, other, own)
    return jnp.stack([first, second], axis)


def lamb_parts(master, first, second, grad):
    next_first = beta_one * first + (1.0 - beta_one) * grad
    next_second = beta_two * second + (1.0 - beta_two) * grad * grad
    ratio = (
        next_first
        / (1.0 - beta_one**step_count)
        / (jnp.sqrt(next_second / (1.0 - beta_two**step_count)) + adam_eps)
        + decay_rate * master
    )
    return (next_first, next_second, ratio)


def group_squares(values, axes):
    return jnp.sum(values * values, axis=axes).reshape(-1)


def row_renew(master, ratio):
    weight_norm = jnp.sqrt(jnp.sum(master * master, axis=1, keepdims=True))
    ratio_norm = jnp.sqrt(jnp.sum(ratio * ratio, axis=1, keepdims=True))
    return master - learn_rate * (weight_norm / ratio_norm) * ratio


def body(
    latents,
    skip_input,
    text_states,
    timesteps,
    patch_order,
    out_grad,
    head_inputs,
    first_head_inputs,
    second_head_inputs,
    text_inputs,
    first_text_inputs,
    second_text_inputs,
    head_outputs,
    first_head_outputs,
    second_head_outputs,
    mlp_inner,
    first_mlp_inner,
    second_mlp_inner,
    mlp_outer,
    first_mlp_outer,
    second_mlp_outer,
    skip_linear,
    first_skip_linear,
    second_skip_linear,
    shift_linear,
    first_shift_linear,
    second_shift_linear,
    row_gains,
    first_row_gains,
    second_row_gains,
    head_gains,
    first_head_gains,
    second_head_gains,
):
    dp_count = lax.axis_size("dp")
    tensor_count = lax.axis_size("tensor")
    me_d = lax.axis_index("dp")
    me_t = lax.axis_index("tensor")
    me_y = me_t // 2
    sizes = digits_of(dp_count)
    plane, space = Grid(sizes, False), Grid(sizes, True)
    width = latents.shape[2]
    block = latents.shape[1]
    rows = 2 * block
    depth = width // dp_count
    text_depth = text_inputs.shape[0]
    text_width = text_depth * dp_count
    head_cols = head_inputs.shape[2]
    hidden_cols = mlp_inner.shape[1]
    latent_count = 2 * dp_count

    low_head = head_inputs.astype(BF16)
    low_out = head_outputs.astype(BF16)
    half_depth = skip_linear.shape[0] // 2
    skip_half = lax.dynamic_slice_in_dim(skip_linear, (me_t % 2) * half_depth, half_depth, 0).astype(BF16)
    self_pack = jnp.concatenate([low_head[:, 0:3].reshape(depth, 3 * head_cols), low_out[0].T], 1)
    cross_pack = jnp.concatenate(
        [
            jnp.concatenate([low_head[:, 3], low_out[1].T], 1),
            text_inputs.astype(BF16).reshape(text_depth, 2 * head_cols),
        ],
        0,
    )
    mlp_pack = jnp.concatenate([mlp_inner.astype(BF16), mlp_outer.T.astype(BF16)], 1)

    def mine_first(pair):
        return (
            lax.dynamic_index_in_dim(pair, me_y, 0, keepdims=False),
            lax.dynamic_index_in_dim(pair, 1 - me_y, 0, keepdims=False),
        )

    def by_latent(own, other):
        return jnp.where(me_y == 0, jnp.stack([own, other]), jnp.stack([other, own]))

    joined_own, joined_other = mine_first(jnp.concatenate([latents, skip_input], -1))
    joined_got = swap_y(joined_other)
    joined16 = jnp.concatenate([joined_own, joined_got], 0)
    skip_job, self_job = Fetch(plane, skip_half), Fetch(space, self_pack)
    cross_job, mlp_job = Fetch(space, cross_pack), Fetch(plane, mlp_pack)
    order = Sequence()
    steps = jnp.zeros((dp_count, 2), F32)
    steps = lax.dynamic_update_slice(steps, timesteps.astype(F32)[None], (me_d, 0))
    steps = sum_everywhere(steps, dp_only=True).reshape(latent_count)
    silu16 = jax.nn.silu(time_embed(steps)).astype(BF16)
    silu_cols = lax.dynamic_slice_in_dim(silu16, me_d * depth, depth, 1)
    shifts = sum_everywhere(matmul(silu_cols, shift_linear.astype(BF16)), dp_only=True)
    my_latent = me_d * 2 + me_y
    shift = lax.dynamic_slice_in_dim(shifts, my_latent, 1, 0)
    order.run(skip_job)
    order.run(skip_job, since=(steps,))
    order.run(skip_job)
    order.run(skip_job, since=(shifts,))
    skip_got = skip_job.finish()
    order.run(self_job)
    skip_far = swap_core(skip_got)
    order.run(self_job, since=(skip_far,))
    skip_mat = place([skip_got, skip_far], [me_t % 2, 1 - me_t % 2], 1)
    skip_mat = skip_mat.reshape(2 * width, width)

    places = patch_order.reshape(tensor_count, block)
    places = jnp.concatenate(
        [lax.dynamic_index_in_dim(places, me_t ^ k, 0, keepdims=False) for k in (0, 2, 1, 3)]
    )
    tables = rotary_tables(places)
    gain_pads = jnp.pad(head_gains, ((0, 0), (0, LANES - HD)))
    self_gains = jnp.pad(gain_pads[0:2], ((0, 6), (0, 0)))
    cross_gains = jnp.pad(gain_pads[2:4], ((0, 6), (0, 0)))
    text_part = lax.dynamic_index_in_dim(text_states, me_y, 0, keepdims=False)

    cot_own, cot_other = mine_first(out_grad)
    cot_pair = jnp.concatenate([cot_own, cot_other], 0).astype(BF16)
    cot_got = swap_y(after(cot_pair, *order.came))
    cotangent = jnp.concatenate([cot_own, cot_got[block:].astype(F32)], 0)
    mlp_full_grad = gather_core(
        jnp.concatenate([cot_pair[:block], cot_got[block:], cot_got[:block], cot_pair[block:]], 0)
    )

    skip_gain = row_gains[0:2].reshape(-1)
    normed, normed_back = jax.vjp(norm_rows, joined16.astype(F32), skip_gain)
    normed16 = normed.astype(BF16)
    hidden = matmul(normed16, skip_mat)
    order.run(self_job, cross_job, since=(hidden,))
    first_norm, first_back = jax.vjp(norm_rows, hidden, row_gains[2])
    attn16 = (first_norm + shift).astype(BF16)
    order.run(self_job, cross_job, since=(attn16,))
    order.run(self_job)
    self_got = self_job.finish()
    self_near = self_got[0].reshape(width, 4 * head_cols)
    self_far = self_got[1].reshape(width, 4 * head_cols)
    came = order.run(cross_job, mlp_job, since=(self_got,))
    self_mats = [pack[:, : 3 * head_cols] for pack in (self_near, self_far)]
    self_outs = [pack[:, 3 * head_cols :] for pack in (self_near, self_far)]
    attn_full = gather_core(attn16)
    heads = head_cols // HD
    self_places = (0, head_cols, 2 * head_cols)
    self_pres = [matmul(attn_full, self_mats[0])]
    self_kept = [attend((self_pres[0],), self_gains, tables, heads, self_places, 2 * rows)]
    coming = order.run(cross_job, mlp_job, since=self_kept[0][:1])
    self_pres.append(matmul(after(attn_full, self_kept[0][0], *came), self_mats[1]))
    self_kept.append(attend((self_pres[1],), self_gains, tables, heads, self_places, 2 * rows))
    self_flat = after(self_kept[1][0], *coming)
    order.run(cross_job, mlp_job, since=(self_flat,))
    after_self = hidden + sum_core(
        matmul_nt(self_kept[0][0], self_outs[0]) + matmul_nt(self_flat, self_outs[1])
    )
    third_norm, third_back = jax.vjp(norm_rows, after_self, row_gains[3])
    cross_pair = cross_job.finish()
    cross_mat = jnp.concatenate(
        [cross_pair[k, :, :depth, :head_cols].reshape(width, head_cols) for k in range(2)], 1
    )
    cross_out = jnp.concatenate(
        [cross_pair[k, :, :depth, head_cols:].reshape(width, head_cols) for k in range(2)], 1
    )
    text_mat = jnp.concatenate(
        [cross_pair[k, :, depth:, :head_cols].reshape(text_width, head_cols) for k in range(2)]
        + [cross_pair[k, :, depth:, head_cols:].reshape(text_width, head_cols) for k in range(2)],
        1,
    )
    cross_kept = gather_core(third_norm.astype(BF16))
    came = order.run(mlp_job, since=(cross_kept,))
    text_rows = text_part.shape[0]
    text_pad = jnp.pad(text_part, ((0, -text_rows % LANES), (0, 0)))
    cross_pres = (matmul(cross_kept, cross_mat), matmul(text_pad, text_mat))
    cross_places = (0, 0, 2 * head_cols)
    cross_kept_all = attend(
        cross_pres, cross_gains, tables, 2 * heads, cross_places, text_rows
    )
    cross_flat = cross_kept_all[0]
    after_cross = after_self + sum_core(matmul_nt(after(cross_flat, *came), cross_out))
    second_norm, second_back = jax.vjp(norm_rows, after_cross, row_gains[4])

    mlp16 = second_norm.astype(BF16)
    mlp_got = mlp_job.finish().reshape(width, 2 * hidden_cols)
    mlp_kept = gather_core(jnp.concatenate([mlp16, swap_y(mlp16)], 0))
    activated16, inner_grad16, *shares = mlp_both(mlp_kept, mlp_full_grad, mlp_got)
    out_mine, in_mine, out_theirs, in_theirs = shares

    in_part = add_low(in_mine, swap_core(in_theirs), F32)
    in_got = swap_y(in_part[rows:].astype(BF16))
    mlp_in_grad = in_part[:rows] + in_got.astype(F32)
    inner_wgrad = wgrad(mlp_kept, after(inner_grad16, in_part))
    outer_wgrad = wgrad(mlp_full_grad, after(activated16, in_part))

    def put_back(values):
        got = swap_y(values[block:].astype(BF16))
        return got, by_latent(values[:block], got.astype(F32))


    def rows_of(matrix, dp_index, count):
        return lax.dynamic_slice_in_dim(matrix, dp_index * count, count, 0)

    def mlp_part(at, _):
        return jnp.concatenate([rows_of(inner_wgrad, at, depth), rows_of(outer_wgrad, at, depth)], 1)

    mlp_run = Reduction(plane, mlp_part)
    order = Sequence()
    came = order.run(mlp_run, since=(inner_wgrad, outer_wgrad, in_got))
    cross_res_grad, fifth_gain_grad = second_back(mlp_in_grad)
    after_cross_grad = cotangent + cross_res_grad
    cross_full_grad = gather_core(after_cross_grad.astype(BF16))
    cross_out_wgrad = matmul_tn(cross_full_grad, cross_flat).astype(BF16)
    cross_mixed_grad = matmul(cross_full_grad, cross_out).astype(BF16)
    coming = order.run(mlp_run, since=(cross_mixed_grad,))
    out_part = add_low(out_mine, swap_core(after(out_theirs, cross_mixed_grad)), F32)
    cq_pre16, text_grad16, cross_gain_grad = attend_back(
        cross_pres, after(cross_gains, *came), tables, cross_kept_all, cross_mixed_grad, 2 * heads, cross_places
    )
    came = order.run(mlp_run, since=(cq_pre16,))
    out_got = swap_y(after(out_part[rows:].astype(BF16), cq_pre16))
    result = after_cross + out_part[:rows] + out_got.astype(F32)
    text_wgrad = matmul_tn(text_pad, text_grad16).astype(BF16)
    cross_q_wgrad = matmul_tn(cross_kept, cq_pre16).astype(BF16)

    def cross_part(at, far):
        near = slice(far * head_cols, (far + 1) * head_cols)
        values = slice((2 + far) * head_cols, (3 + far) * head_cols)
        top = [rows_of(grad[:, near], at, depth) for grad in (cross_q_wgrad, cross_out_wgrad)]
        low = [rows_of(text_wgrad[:, columns], at, text_depth) for columns in (near, values)]
        return jnp.concatenate([jnp.concatenate(top, 1), jnp.concatenate(low, 1)], 0)

    cross_run = Reduction(space, cross_part)
    self_res_grad, fourth_gain_grad = third_back(sum_core(matmul_nt(after(cq_pre16, *coming), cross_mat)))
    after_self_grad = after_cross_grad + self_res_grad
    self_full_grad = gather_core(after_self_grad.astype(BF16))
    attn_part = 0.0
    self_gain_grad = 0.0
    coming = order.run(mlp_run, cross_run, since=(self_full_grad,))
    came = came + (out_got,)
    pre16 = self_full_grad
    in_wgrads, out_wgrads = [], []
    for k in range(2):
        mixed_grad = matmul(self_full_grad, self_outs[k]).astype(BF16)
        pre16, gain_grad = attend_back(
            (self_pres[k],),
            after(self_gains, pre16, *came),
            tables,
            self_kept[k],
            mixed_grad,
            heads,
            self_places,
        )
        self_gain_grad = self_gain_grad + gain_grad
        came, coming = coming, order.run(cross_run, since=(pre16,))
        if k == 0:
            result_got, block_out = put_back(after(result, pre16))
        attn_part = attn_part + matmul_nt(pre16, self_mats[k])
        in_wgrads.append(matmul_tn(attn_full, pre16).astype(BF16))
        out_wgrads.append(matmul_tn(self_full_grad, self_kept[k][0]).astype(BF16))

    def self_part(at, far):
        return jnp.concatenate(
            [rows_of(in_wgrads[far], at, depth), rows_of(out_wgrads[far], at, depth)], 1
        )

    self_run = Reduction(space, self_part)
    attn_grad = sum_core(attn_part)
    attn_grad = after(attn_grad, result_got, *came)
    hidden_norm_grad, third_gain_grad = first_back(attn_grad)
    shift_grad = jnp.sum(attn_grad, axis=0)
    order.run(cross_run, self_run, since=(attn_part,))
    order.run(cross_run, self_run, since=(attn_grad,))
    hidden_grad16 = (after_self_grad + hidden_norm_grad).astype(BF16)
    skip_wgrad = matmul_tn(normed16, hidden_grad16).astype(BF16)
    joined_grad, skip_gain_grad = normed_back(matmul_nt(hidden_grad16, skip_mat))
    order.run(self_run)

    skip_parts = skip_wgrad.reshape(dp_count, 2, half_depth, width)
    mine = lax.dynamic_index_in_dim(skip_parts, me_t % 2, 1, keepdims=False)
    theirs = lax.dynamic_index_in_dim(skip_parts, 1 - me_t % 2, 1, keepdims=False)
    skip_parts = add_low(mine, swap_core(theirs))
    skip_run = Reduction(plane, lambda at, _: lax.dynamic_index_in_dim(skip_parts, at, 0, False), BF16)
    order.run(self_run, skip_run)
    order.run(self_run, skip_run)
    order.run(skip_run)
    order.run(skip_run)
    mlp_sum, cross_sum, self_sum = mlp_run.finish(), cross_run.finish(), self_run.finish()
    skip_sum = skip_run.finish()
    skip_sum = add_low(skip_sum, swap_y(skip_sum))
    skip_mat_grad = in_order(skip_sum, swap_core(skip_sum), me_t % 2)
    skip_mat_grad = skip_mat_grad.reshape(2 * half_depth, width).astype(F32)

    row_grad = jnp.stack(
        [
            skip_gain_grad[:width],
            skip_gain_grad[width:],
            third_gain_grad,
            fourth_gain_grad,
            fifth_gain_grad,
        ]
    )
    head_grad = jnp.concatenate([self_gain_grad[0:2, :HD], cross_gain_grad[0:2, :HD]], 0)
    single = jnp.zeros((latent_count, width), F32)
    single = lax.dynamic_update_slice(single, shift_grad[None], (my_latent, 0))
    head_row = jnp.pad(head_grad.reshape(1, -1), ((0, 0), (0, width - head_grad.size)))
    single = sum_everywhere(jnp.concatenate([single, row_grad, head_row], 0))
    row_gain_grad = single[latent_count : latent_count + 5]
    head_gain_grad = single[latent_count + 5, : head_grad.size].reshape(head_grad.shape)
    shift_mat_grad = lax.dot_general(
        silu_cols.astype(F32),
        single[:latent_count],
        (((0,), (0,)), ((), ())),
        precision=lax.Precision.HIGHEST,
        preferred_element_type=F32,
    )

    head_in_grad = jnp.concatenate(
        [
            self_sum[:, : 3 * head_cols].reshape(depth, 3, head_cols),
            cross_sum[:depth, None, :head_cols],
        ],
        1,
    )
    text_in_grad = cross_sum[depth:].reshape(text_depth, 2, head_cols)
    head_out_grad = jnp.stack([self_sum[:, 3 * head_cols :].T, cross_sum[:depth, head_cols:].T])
    mlp_in_grad = mlp_sum[:, :hidden_cols]
    mlp_out_grad = mlp_sum[:, hidden_cols:].T

    _, grad_latents = put_back(joined_grad[:, :width])
    _, grad_skip_input = put_back(joined_grad[:, width:])
    head_in_first, head_in_second, head_in_ratio = lamb_parts(
        head_inputs, first_head_inputs, second_head_inputs, head_in_grad
    )
    text_in_first, text_in_second, text_in_ratio = lamb_parts(
        text_inputs, first_text_inputs, second_text_inputs, text_in_grad
    )
    head_out_first, head_out_second, head_out_ratio = lamb_parts(
        head_outputs, first_head_outputs, second_head_outputs, head_out_grad
    )
    mlp_in_first, mlp_in_second, mlp_in_ratio = lamb_parts(
        mlp_inner, first_mlp_inner, second_mlp_inner, mlp_in_grad
    )
    mlp_out_first, mlp_out_second, mlp_out_ratio = lamb_parts(
        mlp_outer, first_mlp_outer, second_mlp_outer, mlp_out_grad
    )
    skip_mat_first, skip_mat_second, skip_mat_ratio = lamb_parts(
        skip_linear, first_skip_linear, second_skip_linear, skip_mat_grad
    )
    shift_mat_first, shift_mat_second, shift_mat_ratio = lamb_parts(
        shift_linear, first_shift_linear, second_shift_linear, shift_mat_grad
    )
    weight_squares = jnp.concatenate(
        [
            group_squares(head_inputs, (0, 2)),
            group_squares(text_inputs, (0, 2)),
            group_squares(head_outputs, (1, 2)),
            group_squares(mlp_inner, (0, 1)),
            group_squares(mlp_outer, (0, 1)),
            group_squares(skip_linear, (0, 1)),
            group_squares(shift_linear, (0, 1)),
        ]
    )
    ratio_squares = jnp.concatenate(
        [
            group_squares(head_in_ratio, (0, 2)),
            group_squares(text_in_ratio, (0, 2)),
            group_squares(head_out_ratio, (1, 2)),
            group_squares(mlp_in_ratio, (0, 1)),
            group_squares(mlp_out_ratio, (0, 1)),
            group_squares(skip_mat_ratio, (0, 1)),
            group_squares(shift_mat_ratio, (0, 1)),
        ]
    )
    weight_squares, ratio_squares = sum_everywhere(jnp.stack([weight_squares, ratio_squares]))
    correction = jnp.concatenate(
        [jnp.ones((10,), jnp.float32), jnp.full((2,), 1.0 / lax.axis_size("tensor"), jnp.float32)]
    )
    weight_norms = jnp.sqrt(weight_squares * correction)
    ratio_norms = jnp.sqrt(ratio_squares * correction)
    trust = weight_norms / ratio_norms
    head_in_new = head_inputs - learn_rate * trust[0:4][None, :, None] * head_in_ratio
    text_in_new = text_inputs - learn_rate * trust[4:6][None, :, None] * text_in_ratio
    head_out_new = head_outputs - learn_rate * trust[6:8][:, None, None] * head_out_ratio
    mlp_in_new = mlp_inner - learn_rate * trust[8] * mlp_in_ratio
    mlp_out_new = mlp_outer - learn_rate * trust[9] * mlp_out_ratio
    skip_mat_new = skip_linear - learn_rate * trust[10] * skip_mat_ratio
    shift_mat_new = shift_linear - learn_rate * trust[11] * shift_mat_ratio
    row_gain_first, row_gain_second, row_gain_ratio = lamb_parts(
        row_gains, first_row_gains, second_row_gains, row_gain_grad
    )
    head_gain_first, head_gain_second, head_gain_ratio = lamb_parts(
        head_gains, first_head_gains, second_head_gains, head_gain_grad
    )
    row_gain_new = row_renew(row_gains, row_gain_ratio)
    head_gain_new = row_renew(head_gains, head_gain_ratio)
    return (
        block_out,
        grad_latents,
        grad_skip_input,
        head_in_grad,
        head_in_first,
        head_in_second,
        head_in_new,
        text_in_grad,
        text_in_first,
        text_in_second,
        text_in_new,
        head_out_grad,
        head_out_first,
        head_out_second,
        head_out_new,
        mlp_in_grad,
        mlp_in_first,
        mlp_in_second,
        mlp_in_new,
        mlp_out_grad,
        mlp_out_first,
        mlp_out_second,
        mlp_out_new,
        skip_mat_grad,
        skip_mat_first,
        skip_mat_second,
        skip_mat_new,
        shift_mat_grad,
        shift_mat_first,
        shift_mat_second,
        shift_mat_new,
        row_gain_grad,
        row_gain_first,
        row_gain_second,
        row_gain_new,
        head_gain_grad,
        head_gain_first,
        head_gain_second,
        head_gain_new,
        weight_norms,
        ratio_norms,
    )


def solution(mesh):
    return jax.shard_map(
        body,
        mesh=mesh,
        in_specs=(
            P("dp", "tensor", None),
            P("dp", "tensor", None),
            P("dp", None, None),
            P("dp"),
            P(),
            P("dp", "tensor", None),
            P("dp", None, "tensor"),
            P("dp", None, "tensor"),
            P("dp", None, "tensor"),
            P("dp", None, "tensor"),
            P("dp", None, "tensor"),
            P("dp", None, "tensor"),
            P(None, "tensor", "dp"),
            P(None, "tensor", "dp"),
            P(None, "tensor", "dp"),
            P("dp", "tensor"),
            P("dp", "tensor"),
            P("dp", "tensor"),
            P("tensor", "dp"),
            P("tensor", "dp"),
            P("tensor", "dp"),
            P("dp", None),
            P("dp", None),
            P("dp", None),
            P("dp", None),
            P("dp", None),
            P("dp", None),
            P(),
            P(),
            P(),
            P(),
            P(),
            P(),
        ),
        out_specs=(
            P("dp", "tensor", None),
            P("dp", "tensor", None),
            P("dp", "tensor", None),
            P("dp", None, "tensor"),
            P("dp", None, "tensor"),
            P("dp", None, "tensor"),
            P("dp", None, "tensor"),
            P("dp", None, "tensor"),
            P("dp", None, "tensor"),
            P("dp", None, "tensor"),
            P("dp", None, "tensor"),
            P(None, "tensor", "dp"),
            P(None, "tensor", "dp"),
            P(None, "tensor", "dp"),
            P(None, "tensor", "dp"),
            P("dp", "tensor"),
            P("dp", "tensor"),
            P("dp", "tensor"),
            P("dp", "tensor"),
            P("tensor", "dp"),
            P("tensor", "dp"),
            P("tensor", "dp"),
            P("tensor", "dp"),
            P("dp", None),
            P("dp", None),
            P("dp", None),
            P("dp", None),
            P("dp", None),
            P("dp", None),
            P("dp", None),
            P("dp", None),
            P(),
            P(),
            P(),
            P(),
            P(),
            P(),
            P(),
            P(),
            P(),
            P(),
        ),
        check_vma=False,
    )
```

```python
from functools import partial
import itertools
import math

import jax
import jax.numpy as jnp
from jax import lax
from jax.experimental import pallas as pl
from jax.experimental.pallas import tpu as pltpu
from jax.sharding import PartitionSpec as P

D = 1408
HD = 88
GRID = 32


norm_eps = 1e-06
beta_one = 0.9
beta_two = 0.999
adam_eps = 1e-06
decay_rate = 0.01
learn_rate = 0.3
step_count = 10.0

BF16 = jnp.bfloat16
F32 = jnp.float32


def matmul(left, right):
    return jnp.dot(left, right, preferred_element_type=jnp.float32)


def matmul_tn(left, right):
    return lax.dot_general(
        left, right, (((0,), (0,)), ((), ())), preferred_element_type=jnp.float32
    )


def matmul_nt(left, right):
    return lax.dot_general(
        left, right, (((1,), (1,)), ((), ())), preferred_element_type=jnp.float32
    )


def norm_rows(values, factor):
    center = values - jnp.mean(values, axis=-1, keepdims=True)
    spread = jnp.mean(center * center, axis=-1, keepdims=True)
    return center * lax.rsqrt(spread + norm_eps) * factor


def rotary_tables(places):
    grid_row = (places // GRID).astype(jnp.float32)
    grid_col = (places % GRID).astype(jnp.float32)
    quarter = HD // 4
    spacing = 10000.0 ** (-jnp.arange(quarter).astype(jnp.float32) / quarter)
    row_angle = jnp.repeat(grid_row[:, None] * spacing[None, :], 2, axis=1)
    col_angle = jnp.repeat(grid_col[:, None] * spacing[None, :], 2, axis=1)
    angles = jnp.concatenate([row_angle, col_angle], 1)
    even = jnp.arange(HD) % 2 == 0
    sines = jnp.sin(angles)
    tables = (jnp.cos(angles), jnp.where(even, -sines, 0.0), jnp.where(even, 0.0, sines))
    return tuple(jnp.pad(table, ((0, 0), (0, LANES - HD))) for table in tables)


def time_embed(timesteps):
    half_width = D // 2
    spacing = jnp.exp(-math.log(10000.0) * jnp.arange(half_width).astype(jnp.float32) / half_width)
    angles = timesteps.astype(jnp.float32)[:, None] * spacing[None, :]
    return jnp.concatenate([jnp.cos(angles), jnp.sin(angles)], -1)


def gelu_tanh(values):
    return jax.nn.gelu(values, approximate=True)


LANES = 128
Q_SCALE = math.log2(math.e) * HD**-0.5
FAR = -10000.0


def head_slice(ref, at):
    width = ref.shape[1]
    if at + LANES <= width:
        values = ref[:, at : at + LANES]
    else:
        values = pltpu.roll(ref[:, width - LANES :], width - at, 1)
    return jnp.where(lanes_of(values) < HD, values, 0.0)


def lanes_of(values):
    return lax.broadcasted_iota(jnp.int32, values.shape, 1)


def head_norm(pre):
    mean = jnp.sum(pre, axis=1, keepdims=True) * (1.0 / HD)
    center = jnp.where(lanes_of(pre) < HD, pre - mean, 0.0)
    spread = jnp.sum(center * center, axis=1, keepdims=True) * (1.0 / HD)
    scale = lax.rsqrt(spread + norm_eps)
    return center * scale, scale


def turn(values, tables):
    cosines, after, before = (table[...] for table in tables)
    return (
        values * cosines
        + pltpu.roll(values, LANES - 1, 1) * after
        + pltpu.roll(values, 1, 1) * before
    )


def turn_back(grads, tables):
    cosines, after, before = (table[...] for table in tables)
    return (
        grads * cosines
        + pltpu.roll(grads * after, 1, 1)
        + pltpu.roll(grads * before, LANES - 1, 1)
    )


def head_norm_back(grads, gain, normed, scale):
    gain_grad = jnp.sum(grads * normed, axis=0, keepdims=True)
    grads = grads * gain
    mean = jnp.sum(grads, axis=1, keepdims=True) * (1.0 / HD)
    along = jnp.sum(grads * normed, axis=1, keepdims=True) * (1.0 / HD)
    back = scale * (grads - mean - normed * along)
    return jnp.where(lanes_of(back) < HD, back, 0.0), gain_grad


def dot_nt(left, right):
    return lax.dot_general(left, right, (((1,), (1,)), ((), ())), preferred_element_type=F32)


def with_pair(values, column, lanes):
    high = column.astype(BF16).astype(F32)
    return jnp.where(lanes == HD, high, jnp.where(lanes == HD + 1, column - high, values))


def attend_kernel(heads, q_at, k_at, v_at, one_pre, key_rows, *refs):
    if one_pre:
        refs = (refs[0],) + refs
    q_ref, kv_ref, gain_ref, cos_ref, after_ref, before_ref = refs[:6]
    out_ref, q_ext_ref, k_ext_ref, v_ext_ref, flat_ref = refs[6:]
    tables = (cos_ref, after_ref, before_ref)
    rows, keys_count = q_ref.shape[0], kv_ref.shape[0]
    step = min(rows, 256)
    for h in range(heads):
        ext = slice(h * LANES, (h + 1) * LANES)
        normed, _ = head_norm(head_slice(q_ref, q_at + h * HD))
        lanes = lanes_of(normed)
        query = turn(normed * gain_ref[0:1], tables) * Q_SCALE
        query = jnp.where(lanes == HD + 2, FAR, query)
        q_ext_ref[:, ext] = query.astype(BF16)
        normed, _ = head_norm(head_slice(kv_ref, k_at + h * HD))
        keys = normed * gain_ref[1:2]
        if one_pre:
            keys = turn(keys, tables)
        lanes = lanes_of(keys)
        keys = jnp.where((lanes == HD) | (lanes == HD + 1), 1.0, keys)
        if key_rows < keys_count:
            places = lax.broadcasted_iota(jnp.int32, keys.shape, 0)
            keys = jnp.where((lanes == HD + 2) & (places >= key_rows), 1.0, keys)
        keys16 = keys.astype(BF16)
        k_ext_ref[:, ext] = keys16
        values = head_slice(kv_ref, v_at + h * HD)
        values16 = jnp.where((lanes == HD) | (lanes == HD + 1), 1.0, values).astype(BF16)
        v_ext_ref[:, ext] = values16
        for at in range(0, rows, step):
            part = slice(at, at + step)
            query16 = q_ext_ref[part, ext]
            raised = jnp.exp2(dot_nt(query16, keys16)).astype(BF16)
            mixed = jnp.dot(raised, values16, preferred_element_type=F32)
            total = mixed[:, HD : HD + 1]
            mixed = mixed * (1.0 / total)
            flat_ref[part, h * HD : (h + 1) * HD] = mixed[:, :HD]
            query = query16.astype(F32)
            query = with_pair(query, -jnp.log2(total), lanes_of(query))
            q_ext_ref[part, ext] = query.astype(BF16)
    out_ref[...] = flat_ref[...].astype(BF16)


def attend_back_kernel(heads, q_at, k_at, v_at, one_pre, *refs):
    if one_pre:
        refs = (refs[0],) + refs
    q_ref, kv_ref, gain_ref, cos_ref, after_ref, before_ref = refs[:6]
    out_ref, grad_ref, q_ext_ref, k_ext_ref, v_ext_ref = refs[6:11]
    if one_pre:
        pre_grad_ref, gain_grad_ref, flat_ref, out_flat, grad_flat = refs[11:]
        q_flat = kv_flat = flat_ref
    else:
        q_grad_ref, kv_grad_ref, gain_grad_ref, q_flat, kv_flat, out_flat, grad_flat = refs[11:]
    tables = (cos_ref, after_ref, before_ref)
    rows, keys_count = q_ref.shape[0], kv_ref.shape[0]
    step = 256 if keys_count % 256 == 0 else keys_count
    out_flat[...] = out_ref[...].astype(F32)
    grad_flat[...] = grad_ref[...].astype(F32)
    q_gain = jnp.zeros((1, LANES), F32)
    k_gain = jnp.zeros((1, LANES), F32)
    for h in range(heads):
        ext = slice(h * LANES, (h + 1) * LANES)
        grad = head_slice(grad_flat, h * HD)
        delta = jnp.sum(grad * head_slice(out_flat, h * HD), axis=1, keepdims=True)
        grad16 = with_pair(grad, -delta, lanes_of(grad)).astype(BF16)
        query16 = q_ext_ref[:, ext]
        query_grad = jnp.zeros((LANES, rows), F32)
        keys_grad = []
        for at in range(0, keys_count, step):
            part = slice(at, at + step)
            keys16, values16 = k_ext_ref[part, ext], v_ext_ref[part, ext]
            chances = jnp.exp2(dot_nt(keys16, query16))
            score_grad = (chances * dot_nt(values16, grad16)).astype(BF16)
            value_grad = jnp.dot(chances.astype(BF16), grad16, preferred_element_type=F32)
            kv_flat[part, v_at + h * HD : v_at + (h + 1) * HD] = value_grad[:, :HD]
            keys_grad.append(jnp.dot(score_grad, query16, preferred_element_type=F32))
            query_grad = query_grad + lax.dot_general(
                keys16, score_grad, (((0,), (0,)), ((), ())), preferred_element_type=F32
            )
        query_grad = query_grad.T * (HD**-0.5)
        normed, scale = head_norm(head_slice(q_ref, q_at + h * HD))
        query_grad = jnp.where(lanes_of(query_grad) < HD, query_grad, 0.0)
        back, gain_grad = head_norm_back(turn_back(query_grad, tables), gain_ref[0:1], normed, scale)
        q_gain = q_gain + gain_grad
        q_flat[:, q_at + h * HD : q_at + (h + 1) * HD] = back[:, :HD]
        key_grad = jnp.concatenate(keys_grad, 0) * math.log(2.0)
        key_grad = jnp.where(lanes_of(key_grad) < HD, key_grad, 0.0)
        if one_pre:
            key_grad = turn_back(key_grad, tables)
        normed, scale = head_norm(head_slice(kv_ref, k_at + h * HD))
        back, gain_grad = head_norm_back(key_grad, gain_ref[1:2], normed, scale)
        k_gain = k_gain + gain_grad
        kv_flat[:, k_at + h * HD : k_at + (h + 1) * HD] = back[:, :HD]
    gain_grad_ref[...] = jnp.concatenate([q_gain, k_gain, jnp.zeros((6, LANES), F32)], 0)
    if one_pre:
        pre_grad_ref[...] = flat_ref[...].astype(BF16)
    else:
        q_grad_ref[...] = q_flat[...].astype(BF16)
        kv_grad_ref[...] = kv_flat[...].astype(BF16)


VMEM_LIMIT = 60 * 1024 * 1024


def attend(pres, gains, tables, heads, places, key_rows):
    rows, keys_count = pres[0].shape[0], pres[-1].shape[0]
    return pl.pallas_call(
        partial(attend_kernel, heads, *places, len(pres) == 1, key_rows),
        out_shape=(
            jax.ShapeDtypeStruct((rows, heads * HD), BF16),
            jax.ShapeDtypeStruct((rows, heads * LANES), BF16),
            jax.ShapeDtypeStruct((keys_count, heads * LANES), BF16),
            jax.ShapeDtypeStruct((keys_count, heads * LANES), BF16),
        ),
        scratch_shapes=[pltpu.VMEM((rows, heads * HD), F32)],
        compiler_params=pltpu.CompilerParams(vmem_limit_bytes=VMEM_LIMIT),
        cost_estimate=pl.CostEstimate(flops=0, bytes_accessed=0, transcendentals=0),
    )(*pres, gains, *tables)


def attend_back(pres, gains, tables, kept, out_grad, heads, places):
    rows, keys_count = pres[0].shape[0], pres[-1].shape[0]
    return pl.pallas_call(
        partial(attend_back_kernel, heads, *places, len(pres) == 1),
        out_shape=tuple(jax.ShapeDtypeStruct(pre.shape, BF16) for pre in pres)
        + (jax.ShapeDtypeStruct((8, LANES), F32),),
        scratch_shapes=[pltpu.VMEM(pre.shape, F32) for pre in pres]
        + [pltpu.VMEM((rows, heads * HD), F32)] * 2,
        compiler_params=pltpu.CompilerParams(vmem_limit_bytes=VMEM_LIMIT),
        cost_estimate=pl.CostEstimate(flops=0, bytes_accessed=0, transcendentals=0),
    )(*pres, gains, *tables, kept[0], out_grad, *kept[1:])


AXES = ("dp", "tensor")


def digits_of(count):
    found = []
    while count % 4 == 0:
        found.append(4)
        count //= 4
    if count > 1:
        found.append(count)
    return tuple(found)


def send(values, move):
    dp_count, tensor_count = lax.axis_size("dp"), lax.axis_size("tensor")
    pairs = []
    for d in range(dp_count):
        for t in range(tensor_count):
            d2, t2 = move(d, t)
            pairs.append((d * tensor_count + t, d2 * tensor_count + t2))
    return lax.ppermute(values, AXES, pairs)


def swap_core(values):
    return send(values, lambda d, t: (d, t ^ 1))


def swap_y(values):
    return send(values, lambda d, t: (d, t ^ 2))


def after(values, *others):
    return lax.optimization_barrier((values, others))[0]


def plan(sizes):
    nodes = list(itertools.product(*map(range, sizes)))
    have, left, steps = {nodes[0]}, nodes[1:], []

    def ways(node):
        return [ring for ring in range(len(sizes)) if node[ring] and before(node, ring) in have]

    while left:
        step, taken = [], set()
        for ring in range(len(sizes)):
            ready = [node for node in left if node not in taken and ring in ways(node)]
            if ready:
                node = min(ready, key=lambda n: (len(ways(n)), -n[0] if ring == 0 else n[0], n))
                step.append((ring, node))
                taken.add(node)
        have |= taken
        left = [node for node in left if node not in taken]
        steps.append(step)
    return steps


def before(node, ring):
    return node[:ring] + (node[ring] - 1,) + node[ring + 1 :]


class Grid:
    def __init__(self, sizes, with_y):
        self.sizes = sizes
        self.with_y = with_y
        self.strides = [math.prod(sizes[at + 1 :]) for at in range(len(sizes))]
        me = lax.axis_index("dp")
        self.mine = [(me // stride) % size for size, stride in zip(sizes, self.strides)]
        self.steps = plan(sizes + ((2,) if with_y else ()))
        self.nodes = list(itertools.product(*map(range, sizes + ((2,) if with_y else ()))))

    def shift(self, values, ring, by):
        if ring == len(self.sizes):
            return swap_y(values)
        size, stride = self.sizes[ring], self.strides[ring]

        def move(d, t):
            digit = (d // stride) % size
            return (d + ((digit + by) % size - digit) * stride, t)

        return send(values, move)

    def owner(self, node):
        return sum(
            ((mine - far) % size) * stride
            for mine, far, size, stride in zip(self.mine, node, self.sizes, self.strides)
        )


def place_kernel(count, axis, spots_ref, *refs):
    sources, (out_ref, held_ref, in_sems, out_sems) = refs[:count], refs[count:]
    before_axis = (slice(None),) * axis
    reads = [
        pltpu.make_async_copy(source, held_ref.at[k], in_sems.at[k])
        for k, source in enumerate(sources)
    ]
    writes = [
        pltpu.make_async_copy(held_ref.at[k], out_ref.at[before_axis + (spots_ref[k],)], out_sems.at[k])
        for k in range(count)
    ]
    for read in reads:
        read.start()
    for read, write in zip(reads, writes):
        read.wait()
        write.start()
    for write in writes:
        write.wait()


def place(pieces, spots, axis=0):
    count = len(pieces)
    shape = pieces[0].shape
    return pl.pallas_call(
        partial(place_kernel, count, axis),
        out_shape=jax.ShapeDtypeStruct(shape[:axis] + (count,) + shape[axis:], pieces[0].dtype),
        in_specs=[pl.BlockSpec(memory_space=pltpu.SMEM)]
        + [pl.BlockSpec(memory_space=pl.ANY)] * count,
        out_specs=pl.BlockSpec(memory_space=pl.ANY),
        scratch_shapes=[
            pltpu.VMEM((count,) + pieces[0].shape, pieces[0].dtype),
            pltpu.SemaphoreType.DMA((count,)),
            pltpu.SemaphoreType.DMA((count,)),
        ],
        compiler_params=pltpu.CompilerParams(vmem_limit_bytes=VMEM_LIMIT),
        cost_estimate=pl.CostEstimate(flops=0, bytes_accessed=0, transcendentals=0),
    )(jnp.stack([jnp.asarray(spot, jnp.int32) for spot in spots]), *pieces)


class Fetch:
    def __init__(self, grid, piece):
        self.grid = grid
        self.got = {grid.nodes[0]: piece}
        self.small = math.prod(grid.sizes) <= 8
        self.todo = list(grid.steps) if self.small else []

    def advance(self, *waits):
        new = {}
        if self.todo:
            for ring, node in self.todo.pop(0):
                source = self.got[before(node, ring)]
                source = after(source, *waits) if waits else source
                new[node] = self.grid.shift(source, ring, 1)
        self.got.update(new)
        return tuple(new.values())

    def finish(self):
        grid, piece = self.grid, self.got[self.grid.nodes[0]]
        if not self.small:
            whole = lax.all_gather(piece, "dp")
            return jnp.stack([whole, swap_y(whole)]) if grid.with_y else whole
        count = math.prod(grid.sizes)
        spots = [grid.owner(node) + (node[-1] * count if grid.with_y else 0) for node in grid.nodes]
        whole = place([self.got[node] for node in grid.nodes], spots)
        return whole.reshape((2, count) + piece.shape) if grid.with_y else whole


class Sequence:
    def __init__(self):
        self.came = ()

    def run(self, *jobs, since=()):
        waits = self.came + tuple(since)
        self.came = tuple(got for job in jobs for got in job.advance(*waits))
        return self.came


class Reduction:
    def __init__(self, grid, part, last=F32):
        self.grid, self.part, self.last = grid, part, last
        self.small = math.prod(grid.sizes) <= 8
        self.sums = {node: [] for node in grid.nodes}
        self.todo = list(reversed(grid.steps)) if self.small else []

    def total(self, node, dtype):
        dp_index = self.grid.owner(node)
        value = self.part(dp_index, node[-1] if self.grid.with_y else 0).astype(F32)
        for got in self.sums[node]:
            value = value + got.astype(F32)
        return value.astype(dtype)

    def advance(self, *waits):
        came = []
        if self.todo:
            for ring, node in self.todo.pop(0):
                moving = self.total(node, BF16)
                moving = after(moving, *waits) if waits else moving
                got = self.grid.shift(moving, ring, -1)
                self.sums[before(node, ring)].append(got)
                came.append(got)
        return came

    def finish(self):
        while self.todo:
            self.advance()
        if self.small:
            return self.total(self.grid.nodes[0], self.last)
        count = math.prod(self.grid.sizes)
        blocks = []
        for far in range(2 if self.grid.with_y else 1):
            whole = jnp.stack([self.part(k, far) for k in range(count)]).astype(F32)
            whole = lax.psum_scatter(whole, "dp", scatter_dimension=0, tiled=False)
            blocks.append(whole)
        if self.grid.with_y:
            return (blocks[0] + swap_y(blocks[1].astype(BF16)).astype(F32)).astype(self.last)
        return blocks[0].astype(self.last)


def mlp_kernel(half_steps, x_ref, grad_ref, mats_ref, act_ref, inner_grad_ref, *part_refs):
    hidden = act_ref.shape[1]
    inner_mat, outer_mat = mats_ref[:, :hidden], mats_ref[:, hidden:]
    inner = jnp.dot(x_ref[...], inner_mat, preferred_element_type=F32)
    grad = jnp.dot(grad_ref[...], outer_mat, preferred_element_type=F32)
    square = inner * inner
    bend = math.sqrt(2.0 / math.pi)
    turned = jnp.tanh(inner * (bend + (bend * 0.044715) * square))
    rise = 0.5 + 0.5 * turned
    slope = rise + (0.5 * inner) * (1.0 - turned * turned) * (bend + (bend * 3 * 0.044715) * square)
    act_ref[...] = (inner * rise).astype(BF16)
    inner_grad_ref[...] = (grad * slope).astype(BF16)
    out = dot_nt(act_ref[...], outer_mat).astype(BF16)
    in_grad = dot_nt(inner_grad_ref[...], inner_mat).astype(BF16)
    first = pl.program_id(0) < half_steps

    @pl.when(first)
    def _():
        part_refs[0][...] = out
        part_refs[1][...] = in_grad

    @pl.when(jnp.logical_not(first))
    def _():
        part_refs[2][...] = out
        part_refs[3][...] = in_grad


def mlp_both(tokens, grads, mats):
    count, width = tokens.shape
    hidden = mats.shape[1] // 2
    block = 256
    steps = count // block
    half = steps // 2
    row = lambda i: (i, 0)
    mine = lambda i: (jnp.minimum(i, half - 1), 0)
    theirs = lambda i: (jnp.maximum(i - half, 0), 0)
    share = jax.ShapeDtypeStruct((count // 2, width), BF16)
    return pl.pallas_call(
        partial(mlp_kernel, half),
        grid=(steps,),
        in_specs=[
            pl.BlockSpec((block, width), row),
            pl.BlockSpec((block, width), row),
            pl.BlockSpec((width, 2 * hidden), lambda i: (0, 0)),
        ],
        out_specs=[pl.BlockSpec((block, hidden), row)] * 2
        + [pl.BlockSpec((block, width), mine)] * 2
        + [pl.BlockSpec((block, width), theirs)] * 2,
        out_shape=[jax.ShapeDtypeStruct((count, hidden), BF16)] * 2 + [share] * 4,
        compiler_params=pltpu.CompilerParams(vmem_limit_bytes=VMEM_LIMIT),
        cost_estimate=pl.CostEstimate(flops=0, bytes_accessed=0, transcendentals=0),
    )(tokens, grads, mats)


def wgrad_kernel(half, left_ref, right_ref, next_left_ref, next_right_ref, out_ref, turned_ref):
    def part(place, left, right):
        @pl.when(pl.program_id(0) == place)
        def _():
            for at in range(0, left.shape[1], LANES):
                turned_ref[at : at + LANES] = left[:, at : at + LANES].T

        @pl.when((pl.program_id(0) >= place) & (pl.program_id(0) < place + half))
        def _():
            product = jnp.dot(turned_ref[...], right[...], preferred_element_type=F32)
            out_ref[...] = product.astype(BF16)

    part(0, left_ref, right_ref)
    part(half, next_left_ref, next_right_ref)


def wgrad_pair(left, right, next_left, next_right):
    (count, rows), columns = left.shape, right.shape[1]
    block = 512
    half = columns // block
    return pl.pallas_call(
        partial(wgrad_kernel, half),
        grid=(2 * half,),
        in_specs=[
            pl.BlockSpec((count, rows), lambda i: (0, 0)),
            pl.BlockSpec((count, block), lambda i: (0, jnp.minimum(i, half - 1))),
            pl.BlockSpec((count, rows), lambda i: (0, 0)),
            pl.BlockSpec((count, block), lambda i: (0, jnp.maximum(i - half, 0))),
        ],
        out_specs=pl.BlockSpec((rows, block), lambda i: (0, i)),
        out_shape=jax.ShapeDtypeStruct((rows, 2 * columns), BF16),
        scratch_shapes=[pltpu.VMEM((rows, count), BF16)],
        compiler_params=pltpu.CompilerParams(vmem_limit_bytes=VMEM_LIMIT),
        cost_estimate=pl.CostEstimate(flops=0, bytes_accessed=0, transcendentals=0),
    )(left, right, next_left, next_right)


def add_low(left, right, dtype=BF16):
    return (left.astype(F32) + right.astype(F32)).astype(dtype)


def sum_everywhere(values, dp_only=False):
    bit = 1
    if not dp_only:
        while bit < lax.axis_size("tensor"):
            values = values + send(values, lambda d, t: (d, t ^ bit))
            bit *= 2
    bit = 1
    while bit < lax.axis_size("dp"):
        values = values + send(values, lambda d, t: (d ^ bit, t))
        bit *= 2
    return values


def gather_core(rows):
    return jnp.concatenate([rows, swap_core(rows)], 0)


def sum_core(rows):
    half = rows.shape[0] // 2
    return rows[:half] + swap_core(rows[half:].astype(BF16)).astype(F32)


def in_order(own, other, place, axis=0):
    first = jnp.where(place == 0, own, other)
    second = jnp.where(place == 0, other, own)
    return jnp.stack([first, second], axis)


def lamb_parts(master, first, second, grad):
    next_first = beta_one * first + (1.0 - beta_one) * grad
    next_second = beta_two * second + (1.0 - beta_two) * grad * grad
    ratio = (
        next_first
        / (1.0 - beta_one**step_count)
        / (jnp.sqrt(next_second / (1.0 - beta_two**step_count)) + adam_eps)
        + decay_rate * master
    )
    return (next_first, next_second, ratio)


def group_squares(values, axes):
    return jnp.sum(values * values, axis=axes).reshape(-1)


def row_renew(master, ratio):
    weight_norm = jnp.sqrt(jnp.sum(master * master, axis=1, keepdims=True))
    ratio_norm = jnp.sqrt(jnp.sum(ratio * ratio, axis=1, keepdims=True))
    return master - learn_rate * (weight_norm / ratio_norm) * ratio


def body(
    latents,
    skip_input,
    text_states,
    timesteps,
    patch_order,
    out_grad,
    head_inputs,
    first_head_inputs,
    second_head_inputs,
    text_inputs,
    first_text_inputs,
    second_text_inputs,
    head_outputs,
    first_head_outputs,
    second_head_outputs,
    mlp_inner,
    first_mlp_inner,
    second_mlp_inner,
    mlp_outer,
    first_mlp_outer,
    second_mlp_outer,
    skip_linear,
    first_skip_linear,
    second_skip_linear,
    shift_linear,
    first_shift_linear,
    second_shift_linear,
    row_gains,
    first_row_gains,
    second_row_gains,
    head_gains,
    first_head_gains,
    second_head_gains,
):
    dp_count = lax.axis_size("dp")
    tensor_count = lax.axis_size("tensor")
    me_d = lax.axis_index("dp")
    me_t = lax.axis_index("tensor")
    me_y = me_t // 2
    sizes = digits_of(dp_count)
    plane, space = Grid(sizes, False), Grid(sizes, True)
    width = latents.shape[2]
    block = latents.shape[1]
    rows = 2 * block
    depth = width // dp_count
    text_depth = text_inputs.shape[0]
    text_width = text_depth * dp_count
    head_cols = head_inputs.shape[2]
    hidden_cols = mlp_inner.shape[1]
    latent_count = 2 * dp_count

    low_head = head_inputs.astype(BF16)
    low_out = head_outputs.astype(BF16)
    half_depth = skip_linear.shape[0] // 2
    skip_half = lax.dynamic_slice_in_dim(skip_linear, (me_t % 2) * half_depth, half_depth, 0).astype(BF16)
    self_pack = jnp.concatenate([low_head[:, 0:3].reshape(depth, 3 * head_cols), low_out[0].T], 1)
    cross_pack = jnp.concatenate(
        [
            jnp.concatenate([low_head[:, 3], low_out[1].T], 1),
            text_inputs.astype(BF16).reshape(text_depth, 2 * head_cols),
        ],
        0,
    )
    mlp_pack = jnp.concatenate([mlp_inner.astype(BF16), mlp_outer.T.astype(BF16)], 1)

    def mine_first(pair):
        return (
            lax.dynamic_index_in_dim(pair, me_y, 0, keepdims=False),
            lax.dynamic_index_in_dim(pair, 1 - me_y, 0, keepdims=False),
        )

    def by_latent(own, other):
        return jnp.where(me_y == 0, jnp.stack([own, other]), jnp.stack([other, own]))

    joined_own, joined_other = mine_first(jnp.concatenate([latents, skip_input], -1))
    joined_got = swap_y(joined_other)
    joined16 = jnp.concatenate([joined_own, joined_got], 0)
    skip_job, self_job = Fetch(plane, skip_half), Fetch(space, self_pack)
    cross_job, mlp_job = Fetch(space, cross_pack), Fetch(plane, mlp_pack)
    order = Sequence()
    steps = jnp.zeros((dp_count, 2), F32)
    steps = lax.dynamic_update_slice(steps, timesteps.astype(F32)[None], (me_d, 0))
    steps = sum_everywhere(steps, dp_only=True).reshape(latent_count)
    silu16 = jax.nn.silu(time_embed(steps)).astype(BF16)
    silu_cols = lax.dynamic_slice_in_dim(silu16, me_d * depth, depth, 1)
    shifts = sum_everywhere(matmul(silu_cols, shift_linear.astype(BF16)), dp_only=True)
    my_latent = me_d * 2 + me_y
    shift = lax.dynamic_slice_in_dim(shifts, my_latent, 1, 0)
    order.run(skip_job)
    order.run(skip_job, since=(steps,))
    order.run(skip_job, self_job, since=(joined_got,))
    order.run(skip_job, self_job, since=(shifts,))
    skip_got = skip_job.finish()
    order.run(self_job)
    skip_far = swap_core(skip_got)
    order.run(self_job, cross_job, since=(skip_far,))
    skip_mat = place([skip_got, skip_far], [me_t % 2, 1 - me_t % 2], 1)
    skip_mat = skip_mat.reshape(2 * width, width)

    places = patch_order.reshape(tensor_count, block)
    places = jnp.concatenate(
        [lax.dynamic_index_in_dim(places, me_t ^ k, 0, keepdims=False) for k in (0, 2, 1, 3)]
    )
    tables = rotary_tables(places)
    gain_pads = jnp.pad(head_gains, ((0, 0), (0, LANES - HD)))
    self_gains = jnp.pad(gain_pads[0:2], ((0, 6), (0, 0)))
    cross_gains = jnp.pad(gain_pads[2:4], ((0, 6), (0, 0)))
    text_part = lax.dynamic_index_in_dim(text_states, me_y, 0, keepdims=False)

    skip_gain = row_gains[0:2].reshape(-1)
    normed, normed_back = jax.vjp(norm_rows, joined16.astype(F32), skip_gain)
    normed16 = normed.astype(BF16)
    hidden = matmul(normed16, skip_mat)
    order.run(self_job, cross_job, since=(hidden,))
    first_norm, first_back = jax.vjp(norm_rows, hidden, row_gains[2])
    attn16 = (first_norm + shift).astype(BF16)
    order.run(cross_job, since=(attn16,))
    self_got = self_job.finish()
    self_near = self_got[0].reshape(width, 4 * head_cols)
    self_far = self_got[1].reshape(width, 4 * head_cols)
    came = order.run(cross_job, mlp_job, since=(self_got,))

    cot_own, cot_other = mine_first(out_grad)
    cot_pair = jnp.concatenate([cot_own, cot_other], 0).astype(BF16)
    cot_got = swap_y(after(cot_pair, self_got))
    cotangent = jnp.concatenate([cot_own, cot_got[block:].astype(F32)], 0)
    mlp_full_grad = gather_core(
        jnp.concatenate([cot_pair[:block], cot_got[block:], cot_got[:block], cot_pair[block:]], 0)
    )

    self_mats = [pack[:, : 3 * head_cols] for pack in (self_near, self_far)]
    self_outs = [pack[:, 3 * head_cols :] for pack in (self_near, self_far)]
    attn_full = gather_core(attn16)
    heads = head_cols // HD
    self_places = (0, head_cols, 2 * head_cols)
    self_pres = [matmul(attn_full, self_mats[0])]
    self_kept = [attend((self_pres[0],), self_gains, tables, heads, self_places, 2 * rows)]
    coming = order.run(cross_job, mlp_job, since=self_kept[0][:1])
    self_pres.append(matmul(after(attn_full, self_kept[0][0], cot_got, *came), self_mats[1]))
    self_kept.append(attend((self_pres[1],), self_gains, tables, heads, self_places, 2 * rows))
    self_flat = after(self_kept[1][0], *coming)
    after_self = hidden + sum_core(
        matmul_nt(self_kept[0][0], self_outs[0]) + matmul_nt(self_flat, self_outs[1])
    )
    third_norm, third_back = jax.vjp(norm_rows, after_self, row_gains[3])
    cross_pair = cross_job.finish()
    cross_mat = jnp.concatenate(
        [cross_pair[k, :, :depth, :head_cols].reshape(width, head_cols) for k in range(2)], 1
    )
    cross_out = jnp.concatenate(
        [cross_pair[k, :, :depth, head_cols:].reshape(width, head_cols) for k in range(2)], 1
    )
    text_mat = jnp.concatenate(
        [cross_pair[k, :, depth:, :head_cols].reshape(text_width, head_cols) for k in range(2)]
        + [cross_pair[k, :, depth:, head_cols:].reshape(text_width, head_cols) for k in range(2)],
        1,
    )
    cross_kept = gather_core(third_norm.astype(BF16))
    came = order.run(mlp_job, since=(cross_kept,))
    text_rows = text_part.shape[0]
    text_pad = jnp.pad(text_part, ((0, -text_rows % LANES), (0, 0)))
    cross_pres = (matmul(cross_kept, cross_mat), matmul(text_pad, text_mat))
    cross_places = (0, 0, 2 * head_cols)
    cross_kept_all = attend(
        cross_pres, after(cross_gains, mlp_full_grad), tables, 2 * heads, cross_places, text_rows
    )
    cross_flat = cross_kept_all[0]
    after_cross = after_self + sum_core(matmul_nt(after(cross_flat, *came), cross_out))
    second_norm, second_back = jax.vjp(norm_rows, after_cross, row_gains[4])

    mlp16 = second_norm.astype(BF16)
    came = order.run(mlp_job, since=(mlp16,))
    mlp_got = mlp_job.finish().reshape(width, 2 * hidden_cols)
    mlp_kept = gather_core(jnp.concatenate([mlp16, after(swap_y(mlp16), *came)], 0))
    activated16, inner_grad16, *shares = mlp_both(mlp_kept, mlp_full_grad, mlp_got)
    out_mine, in_mine, out_theirs, in_theirs = shares

    in_part = add_low(in_mine, swap_core(in_theirs), F32)
    in_got = swap_y(in_part[rows:].astype(BF16))
    mlp_in_grad = in_part[:rows] + in_got.astype(F32)
    mlp_wgrad = wgrad_pair(
        mlp_kept, after(inner_grad16, in_part), mlp_full_grad, after(activated16, in_part)
    )

    def put_back(values):
        got = swap_y(values[block:].astype(BF16))
        return got, by_latent(values[:block], got.astype(F32))


    def rows_of(matrix, dp_index, count):
        return lax.dynamic_slice_in_dim(matrix, dp_index * count, count, 0)

    def mlp_part(at, _):
        return rows_of(mlp_wgrad, at, depth)

    mlp_run = Reduction(plane, mlp_part)
    order = Sequence()
    came = order.run(mlp_run, since=(mlp_wgrad, in_got))
    cross_res_grad, fifth_gain_grad = second_back(mlp_in_grad)
    after_cross_grad = cotangent + cross_res_grad
    cross_full_grad = gather_core(after_cross_grad.astype(BF16))
    cross_out_wgrad = matmul_tn(cross_full_grad, cross_flat).astype(BF16)
    cross_mixed_grad = matmul(cross_full_grad, cross_out).astype(BF16)
    coming = order.run(mlp_run, since=(cross_mixed_grad,))
    out_part = add_low(out_mine, swap_core(after(out_theirs, cross_mixed_grad)), F32)
    cq_pre16, text_grad16, cross_gain_grad = attend_back(
        cross_pres, after(cross_gains, *came), tables, cross_kept_all, cross_mixed_grad, 2 * heads, cross_places
    )
    text_wgrad = matmul_tn(text_pad, text_grad16).astype(BF16)
    cross_q_wgrad = matmul_tn(cross_kept, cq_pre16).astype(BF16)

    cross_wgrads = []
    for k in range(2):
        near = slice(k * head_cols, (k + 1) * head_cols)
        values = slice((2 + k) * head_cols, (3 + k) * head_cols)
        top = jnp.concatenate([cross_q_wgrad[:, near], cross_out_wgrad[:, near]], 1)
        low = jnp.concatenate([text_wgrad[:, near], text_wgrad[:, values]], 1)
        top = top.reshape(dp_count, depth, 2 * head_cols)
        low = low.reshape(dp_count, text_depth, 2 * head_cols)
        cross_wgrads.append(jnp.concatenate([top, low], 1))
    cross_wgrads = after(tuple(cross_wgrads))

    def cross_part(at, far):
        return lax.dynamic_index_in_dim(cross_wgrads[far], at, 0, keepdims=False)

    cross_run = Reduction(space, cross_part)
    self_res_grad, fourth_gain_grad = third_back(sum_core(matmul_nt(after(cq_pre16, *coming), cross_mat)))
    after_self_grad = after_cross_grad + self_res_grad
    self_full_grad = gather_core(after_self_grad.astype(BF16))
    attn_part = 0.0
    self_gain_grad = 0.0
    coming = order.run(mlp_run, cross_run, since=(self_full_grad,))
    out_got = swap_y(after(out_part[rows:].astype(BF16), self_full_grad))
    result = after_cross + out_part[:rows] + out_got.astype(F32)
    came = ()
    pre16 = self_full_grad
    in_wgrads, out_wgrads = [], []
    for k in range(2):
        mixed_grad = matmul(self_full_grad, self_outs[k]).astype(BF16)
        pre16, gain_grad = attend_back(
            (self_pres[k],),
            after(self_gains, pre16, *came),
            tables,
            self_kept[k],
            mixed_grad,
            heads,
            self_places,
        )
        self_gain_grad = self_gain_grad + gain_grad
        if k == 0:
            came = coming + (out_got,)
            order.run(mlp_run, cross_run, since=(pre16,))
            result_got, block_out = put_back(after(result, pre16))
        attn_part = attn_part + matmul_nt(pre16, self_mats[k])
        in_wgrads.append(matmul_tn(attn_full, pre16).astype(BF16))
        out_wgrads.append(matmul_tn(self_full_grad, self_kept[k][0]).astype(BF16))

    self_wgrads = after(
        tuple(jnp.concatenate([in_wgrads[k], out_wgrads[k]], 1) for k in range(2))
    )

    def self_part(at, far):
        return rows_of(self_wgrads[far], at, depth)

    self_run = Reduction(space, self_part)
    attn_grad = sum_core(attn_part)
    hidden_norm_grad, third_gain_grad = first_back(attn_grad)
    shift_grad = jnp.sum(attn_grad, axis=0)
    hidden_grad16 = (after_self_grad + hidden_norm_grad).astype(BF16)
    skip_wgrad = matmul_tn(normed16, hidden_grad16).astype(BF16)
    joined_grad, skip_gain_grad = normed_back(matmul_nt(hidden_grad16, skip_mat))

    skip_parts = skip_wgrad.reshape(dp_count, 2, half_depth, width)
    mine = lax.dynamic_index_in_dim(skip_parts, me_t % 2, 1, keepdims=False)
    theirs = lax.dynamic_index_in_dim(skip_parts, 1 - me_t % 2, 1, keepdims=False)
    skip_parts = add_low(mine, swap_core(theirs))
    skip_run = Reduction(plane, lambda at, _: lax.dynamic_index_in_dim(skip_parts, at, 0, False), BF16)
    order.run(cross_run, self_run, skip_run, since=(skip_parts, result_got))
    for _ in range(4):
        order.run(cross_run, self_run, skip_run)
    mlp_sum, cross_sum, self_sum = mlp_run.finish(), cross_run.finish(), self_run.finish()
    skip_sum = skip_run.finish()
    skip_sum = add_low(skip_sum, swap_y(skip_sum))
    skip_mat_grad = in_order(skip_sum, swap_core(skip_sum), me_t % 2)
    skip_mat_grad = skip_mat_grad.reshape(2 * half_depth, width).astype(F32)

    row_grad = jnp.stack(
        [
            skip_gain_grad[:width],
            skip_gain_grad[width:],
            third_gain_grad,
            fourth_gain_grad,
            fifth_gain_grad,
        ]
    )
    head_grad = jnp.concatenate([self_gain_grad[0:2, :HD], cross_gain_grad[0:2, :HD]], 0)
    single = jnp.zeros((latent_count, width), F32)
    single = lax.dynamic_update_slice(single, shift_grad[None], (my_latent, 0))
    head_row = jnp.pad(head_grad.reshape(1, -1), ((0, 0), (0, width - head_grad.size)))
    single = sum_everywhere(jnp.concatenate([single, row_grad, head_row], 0))
    row_gain_grad = single[latent_count : latent_count + 5]
    head_gain_grad = single[latent_count + 5, : head_grad.size].reshape(head_grad.shape)
    shift_mat_grad = lax.dot_general(
        silu_cols.astype(F32),
        single[:latent_count],
        (((0,), (0,)), ((), ())),
        precision=lax.Precision.HIGHEST,
        preferred_element_type=F32,
    )

    head_in_grad = jnp.concatenate(
        [
            self_sum[:, : 3 * head_cols].reshape(depth, 3, head_cols),
            cross_sum[:depth, None, :head_cols],
        ],
        1,
    )
    text_in_grad = cross_sum[depth:].reshape(text_depth, 2, head_cols)
    head_out_grad = jnp.stack([self_sum[:, 3 * head_cols :].T, cross_sum[:depth, head_cols:].T])
    mlp_in_grad = mlp_sum[:, :hidden_cols]
    mlp_out_grad = mlp_sum[:, hidden_cols:].T

    _, grad_latents = put_back(joined_grad[:, :width])
    _, grad_skip_input = put_back(joined_grad[:, width:])
    head_in_first, head_in_second, head_in_ratio = lamb_parts(
        head_inputs, first_head_inputs, second_head_inputs, head_in_grad
    )
    text_in_first, text_in_second, text_in_ratio = lamb_parts(
        text_inputs, first_text_inputs, second_text_inputs, text_in_grad
    )
    head_out_first, head_out_second, head_out_ratio = lamb_parts(
        head_outputs, first_head_outputs, second_head_outputs, head_out_grad
    )
    mlp_in_first, mlp_in_second, mlp_in_ratio = lamb_parts(
        mlp_inner, first_mlp_inner, second_mlp_inner, mlp_in_grad
    )
    mlp_out_first, mlp_out_second, mlp_out_ratio = lamb_parts(
        mlp_outer, first_mlp_outer, second_mlp_outer, mlp_out_grad
    )
    skip_mat_first, skip_mat_second, skip_mat_ratio = lamb_parts(
        skip_linear, first_skip_linear, second_skip_linear, skip_mat_grad
    )
    shift_mat_first, shift_mat_second, shift_mat_ratio = lamb_parts(
        shift_linear, first_shift_linear, second_shift_linear, shift_mat_grad
    )
    weight_squares = jnp.concatenate(
        [
            group_squares(head_inputs, (0, 2)),
            group_squares(text_inputs, (0, 2)),
            group_squares(head_outputs, (1, 2)),
            group_squares(mlp_inner, (0, 1)),
            group_squares(mlp_outer, (0, 1)),
            group_squares(skip_linear, (0, 1)),
            group_squares(shift_linear, (0, 1)),
        ]
    )
    ratio_squares = jnp.concatenate(
        [
            group_squares(head_in_ratio, (0, 2)),
            group_squares(text_in_ratio, (0, 2)),
            group_squares(head_out_ratio, (1, 2)),
            group_squares(mlp_in_ratio, (0, 1)),
            group_squares(mlp_out_ratio, (0, 1)),
            group_squares(skip_mat_ratio, (0, 1)),
            group_squares(shift_mat_ratio, (0, 1)),
        ]
    )
    weight_squares, ratio_squares = sum_everywhere(jnp.stack([weight_squares, ratio_squares]))
    correction = jnp.concatenate(
        [jnp.ones((10,), jnp.float32), jnp.full((2,), 1.0 / lax.axis_size("tensor"), jnp.float32)]
    )
    weight_norms = jnp.sqrt(weight_squares * correction)
    ratio_norms = jnp.sqrt(ratio_squares * correction)
    trust = weight_norms / ratio_norms
    head_in_new = head_inputs - learn_rate * trust[0:4][None, :, None] * head_in_ratio
    text_in_new = text_inputs - learn_rate * trust[4:6][None, :, None] * text_in_ratio
    head_out_new = head_outputs - learn_rate * trust[6:8][:, None, None] * head_out_ratio
    mlp_in_new = mlp_inner - learn_rate * trust[8] * mlp_in_ratio
    mlp_out_new = mlp_outer - learn_rate * trust[9] * mlp_out_ratio
    skip_mat_new = skip_linear - learn_rate * trust[10] * skip_mat_ratio
    shift_mat_new = shift_linear - learn_rate * trust[11] * shift_mat_ratio
    row_gain_first, row_gain_second, row_gain_ratio = lamb_parts(
        row_gains, first_row_gains, second_row_gains, row_gain_grad
    )
    head_gain_first, head_gain_second, head_gain_ratio = lamb_parts(
        head_gains, first_head_gains, second_head_gains, head_gain_grad
    )
    row_gain_new = row_renew(row_gains, row_gain_ratio)
    head_gain_new = row_renew(head_gains, head_gain_ratio)
    return (
        block_out,
        grad_latents,
        grad_skip_input,
        head_in_grad,
        head_in_first,
        head_in_second,
        head_in_new,
        text_in_grad,
        text_in_first,
        text_in_second,
        text_in_new,
        head_out_grad,
        head_out_first,
        head_out_second,
        head_out_new,
        mlp_in_grad,
        mlp_in_first,
        mlp_in_second,
        mlp_in_new,
        mlp_out_grad,
        mlp_out_first,
        mlp_out_second,
        mlp_out_new,
        skip_mat_grad,
        skip_mat_first,
        skip_mat_second,
        skip_mat_new,
        shift_mat_grad,
        shift_mat_first,
        shift_mat_second,
        shift_mat_new,
        row_gain_grad,
        row_gain_first,
        row_gain_second,
        row_gain_new,
        head_gain_grad,
        head_gain_first,
        head_gain_second,
        head_gain_new,
        weight_norms,
        ratio_norms,
    )


def solution(mesh):
    return jax.shard_map(
        body,
        mesh=mesh,
        in_specs=(
            P("dp", "tensor", None),
            P("dp", "tensor", None),
            P("dp", None, None),
            P("dp"),
            P(),
            P("dp", "tensor", None),
            P("dp", None, "tensor"),
            P("dp", None, "tensor"),
            P("dp", None, "tensor"),
            P("dp", None, "tensor"),
            P("dp", None, "tensor"),
            P("dp", None, "tensor"),
            P(None, "tensor", "dp"),
            P(None, "tensor", "dp"),
            P(None, "tensor", "dp"),
            P("dp", "tensor"),
            P("dp", "tensor"),
            P("dp", "tensor"),
            P("tensor", "dp"),
            P("tensor", "dp"),
            P("tensor", "dp"),
            P("dp", None),
            P("dp", None),
            P("dp", None),
            P("dp", None),
            P("dp", None),
            P("dp", None),
            P(),
            P(),
            P(),
            P(),
            P(),
            P(),
        ),
        out_specs=(
            P("dp", "tensor", None),
            P("dp", "tensor", None),
            P("dp", "tensor", None),
            P("dp", None, "tensor"),
            P("dp", None, "tensor"),
            P("dp", None, "tensor"),
            P("dp", None, "tensor"),
            P("dp", None, "tensor"),
            P("dp", None, "tensor"),
            P("dp", None, "tensor"),
            P("dp", None, "tensor"),
            P(None, "tensor", "dp"),
            P(None, "tensor", "dp"),
            P(None, "tensor", "dp"),
            P(None, "tensor", "dp"),
            P("dp", "tensor"),
            P("dp", "tensor"),
            P("dp", "tensor"),
            P("dp", "tensor"),
            P("tensor", "dp"),
            P("tensor", "dp"),
            P("tensor", "dp"),
            P("tensor", "dp"),
            P("dp", None),
            P("dp", None),
            P("dp", None),
            P("dp", None),
            P("dp", None),
            P("dp", None),
            P("dp", None),
            P("dp", None),
            P(),
            P(),
            P(),
            P(),
            P(),
            P(),
            P(),
            P(),
            P(),
            P(),
        ),
        check_vma=False,
    )
```
